32 devices in a mesh: pipe: 8 (over z, y), dp: 2 (over x), mp: 2 (over core).
Axes of the slice: x: 2, y: 2, z: 4, core: 2. Of those that a mesh axis runs over, the one named last changes fastest.
Arguments:
- activations: bfloat16 [2, 128, 7168], P('dp', 'pipe', 'mp'), may hold values from -6 to 6
- cotangent: bfloat16 [2, 128, 7168], P('dp', 'pipe', 'mp'), may hold values from -6 to 6
- squeeze_old: bfloat16 [8, 7168, 64], P('pipe', 'mp'), may hold values from -5 to 5
- expand_old: bfloat16 [8, 64, 7168], P('pipe', None, 'mp'), may hold values from -5 to 5
- squeeze_late: bfloat16 [2, 8, 7168, 64], P('dp', 'pipe', 'mp'), may hold values from -6 to 6
- expand_late: bfloat16 [2, 8, 64, 7168], P('dp', 'pipe', None, 'mp'), may hold values from -6 to 6
- stash_inputs: bfloat16 [2, 8, 8, 16, 7168], P('dp', 'pipe', None, None, 'mp'), may hold values from -6 to 6
- forward_in: bfloat16 [2, 8, 16, 7168], P('dp', 'pipe', None, 'mp'), may hold values from -6 to 6
- backward_in: bfloat16 [2, 8, 16, 7168], P('dp', 'pipe', None, 'mp'), may hold values from -6 to 6
Outputs:
- squeeze_new: bfloat16 [8, 7168, 64], P('pipe', 'mp')
- expand_new: bfloat16 [8, 64, 7168], P('pipe', None, 'mp')
- squeeze_grad: bfloat16 [2, 8, 7168, 64], P('dp', 'pipe', 'mp')
- expand_grad: bfloat16 [2, 8, 64, 7168], P('dp', 'pipe', None, 'mp')
- forward_carry: bfloat16 [2, 8, 16, 7168], P('dp', 'pipe', None, 'mp')
- backward_carry: bfloat16 [2, 8, 16, 7168], P('dp', 'pipe', None, 'mp')
The draws below stay inside these ranges and needn't reach their ends.
All inputs are finite; a program needn't handle non-finite values.
Results may differ from the reference program's by a relative error of at most 0.009.
Values may be sent and summed in bfloat16 or wider, within the bound.
No kernel may reach another device: no remote copies, remote signals or barrier semaphores. Data moves between devices by JAX's collectives and lax.ppermute only.
A program may use at most 64 MiB of HBM per device.

```python
import math
import jax
import jax.numpy as jnp
from jax import lax

D = 7168
RANK = 64
ROWS = 16
TICKS = 8
TOK_REP = 128
LAYERS = 8
N_DP = 2


def levels(rng, shape, pieces, smallest, top_value):
    gain = 1.0
    for dim, parts in pieces:
        draws = jax.random.uniform(jax.random.fold_in(jax.random.fold_in(rng, 6), dim), (parts,), jnp.float32, smallest / len(pieces), top_value / len(pieces))
        gain = gain * jnp.repeat(jnp.exp(draws), shape[dim] // parts).reshape((-1,) + (1,) * (len(shape) - 1 - dim))
    return gain


def noise(key, extent, spread, limit, split=(), kind=jnp.bfloat16):
    gain = levels(key, extent, split, -0.22, 0.18) if split else 1.0
    array = jax.random.normal(key, extent, jnp.float32) * spread * gain
    return jnp.minimum(jnp.maximum(array, -limit), limit).astype(kind)


def setup_inputs(seed: int = 0) -> dict:
    key_of = jax.random.split(jax.random.key(seed), 10)
    activations = noise(key_of[0], (N_DP, TOK_REP, D), 1.0, 6.0, ((0, 2), (1, 8), (2, 2)))
    cotangent = noise(key_of[1], (N_DP, TOK_REP, D), 1.0, 6.0, ((0, 2), (1, 8), (2, 2)))
    squeeze_old = noise(key_of[2], (LAYERS, D, RANK), 1.0, 5.0, ((0, 8), (1, 2)))
    expand_old = noise(key_of[3], (LAYERS, RANK, D), 1.0, 5.0, ((0, 8), (2, 2)))
    squeeze_late = noise(key_of[4], (N_DP, LAYERS, D, RANK), 1.0, 6.0, ((0, 2), (1, 8), (2, 2)))
    expand_late = noise(key_of[5], (N_DP, LAYERS, RANK, D), 1.0, 6.0, ((0, 2), (1, 8), (3, 2)))
    stash_inputs = noise(key_of[6], (N_DP, LAYERS, TICKS, ROWS, D), 1.0, 6.0, ((0, 2), (1, 8), (4, 2)))
    forward_in = noise(key_of[7], (N_DP, LAYERS, ROWS, D), 1.0, 6.0, ((0, 2), (1, 8), (3, 2)))
    backward_in = noise(key_of[8], (N_DP, LAYERS, ROWS, D), 1.0, 6.0, ((0, 2), (1, 8), (3, 2)))
    return {"activations": activations, "cotangent": cotangent, "squeeze_old": squeeze_old, "expand_old": expand_old, "squeeze_late": squeeze_late, "expand_late": expand_late, "stash_inputs": stash_inputs, "forward_in": forward_in, "backward_in": backward_in}


BRANCH_SCALE = 0.25
STEP_RATE = 0.5

def activate(values):
    return jax.nn.gelu(values, approximate=True)

def section_forward(inputs, squeeze_old, expand_old):
    inv_width = 1.0 / math.sqrt(D)
    inv_rank = BRANCH_SCALE / math.sqrt(RANK)
    hidden = jnp.einsum('srd,sdk->srk', inputs.astype(jnp.float32), squeeze_old.astype(jnp.float32)) * inv_width
    gated = activate(hidden).astype(jnp.bfloat16)
    branch = jnp.einsum('srk,skd->srd', gated.astype(jnp.float32), expand_old.astype(jnp.float32)) * inv_rank
    return (inputs.astype(jnp.float32) + branch).astype(jnp.bfloat16)

def section_backward(saved, upstream, squeeze_old, expand_old):
    inv_width = 1.0 / math.sqrt(D)
    inv_rank = BRANCH_SCALE / math.sqrt(RANK)
    again = jnp.einsum('srd,sdk->srk', saved.astype(jnp.float32), squeeze_old.astype(jnp.float32)) * inv_width
    gate_grad = jnp.einsum('srd,skd->srk', upstream.astype(jnp.float32), expand_old.astype(jnp.float32)) * inv_rank
    regated, pullback = jax.vjp(activate, again)
    hidden_grad = pullback(gate_grad)[0].astype(jnp.bfloat16)
    regated = regated.astype(jnp.bfloat16)
    expand_term = jnp.einsum('srk,srd->skd', regated.astype(jnp.float32), upstream.astype(jnp.float32)) * inv_rank
    squeeze_term = jnp.einsum('srd,srk->sdk', saved.astype(jnp.float32), hidden_grad.astype(jnp.float32)) * inv_width
    back = jnp.einsum('srk,sdk->srd', hidden_grad.astype(jnp.float32), squeeze_old.astype(jnp.float32)) * inv_width
    downstream = (upstream.astype(jnp.float32) + back).astype(jnp.bfloat16)
    return (downstream, squeeze_term, expand_term)

def replica_pass(feeds, targets, stash, first_fwd, first_bwd, squeeze_old, expand_old):
    section_ids = jnp.arange(LAYERS, dtype=jnp.int32)
    lags = (2 * LAYERS - 1 - 2 * section_ids).astype(jnp.int32)
    squeeze_sum = jnp.zeros((LAYERS, D, RANK), jnp.float32)
    expand_sum = jnp.zeros((LAYERS, RANK, D), jnp.float32)
    history = []
    outputs = None
    downstream = None
    for tick in range(TICKS):
        fed = feeds[tick * ROWS:(tick + 1) * ROWS][None]
        target = targets[tick * ROWS:(tick + 1) * ROWS][None]
        if tick == 0:
            layer_in = jnp.concatenate([fed, first_fwd[1:]], axis=0)
            upstream = jnp.concatenate([first_bwd[:-1], target], axis=0)
        else:
            layer_in = jnp.concatenate([fed, outputs[:-1]], axis=0)
            upstream = jnp.concatenate([downstream[1:], target], axis=0)
        history.append(layer_in)
        outputs = section_forward(layer_in, squeeze_old, expand_old)
        stacked = jnp.stack(history)
        back = (tick - lags).astype(jnp.int32)
        picked = stacked[jnp.clip(back, 0, tick).astype(jnp.int32), section_ids]
        saved = jnp.where((back >= 0)[:, None, None], picked, stash[:, tick])
        downstream, squeeze_term, expand_term = section_backward(saved, upstream, squeeze_old, expand_old)
        squeeze_sum = squeeze_sum + squeeze_term
        expand_sum = expand_sum + expand_term
    return (squeeze_sum.astype(jnp.bfloat16), expand_sum.astype(jnp.bfloat16), outputs, downstream)

def reference(activations, cotangent, squeeze_old, expand_old, squeeze_late, expand_late, stash_inputs, forward_in, backward_in):
    squeeze_new = (squeeze_old.astype(jnp.float32) - STEP_RATE * lax.optimization_barrier(jnp.sum(squeeze_late.astype(jnp.float32), axis=0)) / N_DP).astype(jnp.bfloat16)
    expand_new = (expand_old.astype(jnp.float32) - STEP_RATE * lax.optimization_barrier(jnp.sum(expand_late.astype(jnp.float32), axis=0)) / N_DP).astype(jnp.bfloat16)

    def one_replica(group):
        return replica_pass(group[0], group[1], group[2], group[3], group[4], squeeze_old, expand_old)
    squeeze_grad, expand_grad, forward_carry, backward_carry = lax.map(one_replica, (activations, cotangent, stash_inputs, forward_in, backward_in))
    return (squeeze_new, expand_new, squeeze_grad, expand_grad, forward_carry, backward_carry)
```

```python
import functools
import math

import jax
import jax.numpy as jnp
from jax import lax
from jax.experimental import pallas as pl
from jax.experimental.pallas import tpu as pltpu
from jax.sharding import PartitionSpec as P

BRANCH_SCALE = 0.25
STEP_RATE = 0.5
CHUNK = 512

VMEM = pl.BlockSpec(memory_space=pltpu.VMEM)
SMEM = pl.BlockSpec(memory_space=pltpu.SMEM)
ANY = pl.BlockSpec(memory_space=pl.ANY)
NT = (((1,), (1,)), ((), ()))
TN = (((0,), (0,)), ((), ()))


def dot(a, b, dims=(((1,), (0,)), ((), ()))):
    return lax.dot_general(a, b, dims, preferred_element_type=jnp.float32)


def gelu_and_slope(x):
    c = math.sqrt(2.0 / math.pi)
    t = jnp.tanh(c * (x + 0.044715 * (x * x * x)))
    half = 0.5 * (1.0 + t)
    slope = half + 0.5 * x * (1.0 - t * t) * (c * (1.0 + 3 * 0.044715 * (x * x)))
    return x * half, slope


def split_words(x):
    hi = x.astype(jnp.bfloat16)
    lo = (x - hi.astype(jnp.float32)).astype(jnp.bfloat16)
    return jnp.concatenate([hi, lo], axis=1)


def join_words(words):
    rank = words.shape[1] // 2
    return words[:, :rank].astype(jnp.float32) + words[:, rank:].astype(jnp.float32)


def start_kernel(scale, where, stash, squeeze, fwd, bwd, message, partial):
    ticks, rows, half = stash.shape
    rank = squeeze.shape[0]
    forward = where[1] == 0
    message[:, :half] = jnp.where(forward, bwd[...], fwd[...])
    whole = dot(stash[...].reshape(ticks * rows, half), squeeze[...], NT) * scale
    for t in range(ticks):
        own = whole[t * rows : (t + 1) * rows]
        partial[t] = own
        message[:, half + t * 2 * rank : half + (t + 1) * 2 * rank] = split_words(own)


def tick_kernel(tick, ticks, slots, in_scale, out_scale, where, x_in, feed, again_stash, own, other, *rest):
    mine_in, other_in, out, hist_mine, hist_other, keep_mine, keep_other, sems = rest
    del mine_in, other_in
    rows, half = x_in.shape[0], own.shape[2]
    rank = own.shape[1]
    section, role, sections = where[0], where[1], where[2]
    forward = role == 0
    back = sections - 1 - section
    at_end = jnp.where(forward, section, back) == 0
    x0 = jnp.where(at_end, feed[:, :half], x_in[:, :half])
    x1 = jnp.where(at_end, feed[:, half:], x_in[:, half : 2 * half])
    keep_mine[...] = x0
    keep_other[0, :, :half] = x1
    first = pltpu.make_async_copy(keep_mine, hist_mine.at[tick], sems.at[0])
    first.start()
    h = (dot(x0, own[role], NT) + dot(x1, other[role], NT)) * jnp.where(forward, in_scale, out_scale)
    again = again_stash[tick]
    for j in range(slots):
        if 2 * j + 1 <= tick:
            words = x_in[:, 2 * half + j * 2 * rank : 2 * half + (j + 1) * 2 * rank]
            again = jnp.where(back == j, join_words(words), again)
    value, slope = gelu_and_slope(jnp.where(forward, h, again))
    z = jnp.where(forward, value, h * slope).astype(jnp.bfloat16)
    keep_other[0, :, half:] = jnp.concatenate([value.astype(jnp.bfloat16), z], axis=1)
    scale = jnp.where(forward, out_scale, in_scale)
    y0 = (x0.astype(jnp.float32) + dot(z, own[1 - role]) * scale).astype(jnp.bfloat16)
    y1 = (x1.astype(jnp.float32) + dot(z, other[1 - role]) * scale).astype(jnp.bfloat16)
    out[:, :half] = y0
    if tick + 1 < ticks:
        out[:, half : 2 * half] = y1
        words = split_words(h)
        for j in range(slots):
            place = slice(2 * half + j * 2 * rank, 2 * half + (j + 1) * 2 * rank)
            out[:, place] = jnp.where(jnp.logical_and(forward, back == j), words, x_in[:, place])
        second = pltpu.make_async_copy(keep_other, hist_other.at[pl.ds(tick, 1)], sems.at[1])
    else:
        keep_other[1, :, :half] = y1
        keep_other[1, :, half:] = jnp.zeros((rows, 2 * rank), jnp.bfloat16)
        second = pltpu.make_async_copy(keep_other, hist_other.at[pl.ds(tick, 2)], sems.at[1])
    second.start()
    first.wait()
    second.wait()


def end_kernel(in_scale, out_scale, where, mine, sent, got, stash, carry, squeeze_grad, expand_grad, fwd, bwd):
    ticks, rows, half = mine.shape
    rank = squeeze_grad.shape[0]
    section, role, sections = where[0], where[1], where[2]
    forward = role == 0
    lag = 2 * (sections - 1 - section) + 1
    ranks = jnp.concatenate(
        [jnp.where(forward, got[t, :, half:], sent[t, :, half:]) for t in range(ticks)], axis=0
    )
    regated, hidden_grad = ranks[:, :rank], ranks[:, rank:]
    for lo in range(0, half, CHUNK):
        cols = slice(lo, min(lo + CHUNK, half))
        u, g = [], []
        for t in range(ticks):
            g.append(jnp.where(forward, got[t, :, cols], mine[t, :, cols]))
            back = jnp.maximum(t - lag, 0)
            a = jnp.where(forward, mine[back, :, cols], got[back, :, cols])
            u.append(jnp.where(t >= lag, a, stash[t, :, cols]))
        u, g = jnp.concatenate(u, axis=0), jnp.concatenate(g, axis=0)
        squeeze_grad[:, cols] = (dot(hidden_grad, u, TN) * in_scale).astype(jnp.bfloat16)
        expand_grad[:, cols] = (dot(regated, g, TN) * out_scale).astype(jnp.bfloat16)
    fwd[...] = jnp.where(forward, carry[...], got[ticks, :, :half])
    bwd[...] = jnp.where(forward, got[ticks, :, :half], carry[...])


def params(**more):
    return pltpu.CompilerParams(vmem_limit_bytes=24 * 1024 * 1024, **more)


def cost(flops, nbytes):
    return pl.CostEstimate(flops=flops, bytes_accessed=nbytes, transcendentals=0)


def shards(
    activations,
    cotangent,
    squeeze_old,
    expand_old,
    squeeze_late,
    expand_late,
    stash_inputs,
    forward_in,
    backward_in,
):
    sections = lax.axis_size("pipe")
    replicas = lax.axis_size("dp")
    section = lax.axis_index("pipe")
    role = lax.axis_index("mp")
    half = squeeze_old.shape[1]
    rank = squeeze_old.shape[2]
    ticks, rows = stash_inputs.shape[2], stash_inputs.shape[3]
    width = half * lax.axis_size("mp")
    in_scale = 1.0 / math.sqrt(width)
    out_scale = BRANCH_SCALE / math.sqrt(rank)
    slots = ticks // 2
    bf16, f32 = jnp.bfloat16, jnp.float32

    def send(x, pairs):
        return lax.ppermute(x, ("pipe", "mp"), [(a * 2 + b, c * 2 + d) for (a, b), (c, d) in pairs])

    def swap(x):
        return lax.ppermute(x, "mp", [(0, 1), (1, 0)])

    def shape(*dims, dtype=bf16):
        return jax.ShapeDtypeStruct(dims, dtype)

    where = jnp.stack([section, role, jnp.int32(sections)]).astype(jnp.int32)
    forward = role == 0
    squeeze = squeeze_old[0].T
    expand = expand_old[0]
    stash = stash_inputs[0, 0]
    fwd_in, bwd_in = forward_in[0, 0], backward_in[0, 0]
    acts, cots = activations[0], cotangent[0]

    own = jnp.stack([squeeze, expand])
    other = swap(own)
    entering = jnp.where(forward, acts, cots)
    entering_full = jnp.concatenate([entering, swap(jnp.where(forward, cots, acts))], axis=1)

    message, partial = pl.pallas_call(
        functools.partial(start_kernel, in_scale),
        out_shape=(shape(rows, half + ticks * 2 * rank), shape(ticks, rows, rank, dtype=f32)),
        in_specs=[SMEM, VMEM, VMEM, VMEM, VMEM],
        out_specs=(VMEM, VMEM),
        compiler_params=params(),
        cost_estimate=cost(2 * ticks * rows * half * rank, ticks * rows * half * 2),
        name="start",
    )(where, stash, squeeze, fwd_in, bwd_in)
    got = swap(message)
    words = got[:, half:].reshape(rows, ticks, 2 * rank).transpose(1, 0, 2)
    again_stash = partial + words[..., :rank].astype(f32) + words[..., rank:].astype(f32)

    block = acts.shape[0]
    per_tick = rows // block
    last = sections - 1

    def piece(i, tied):
        pairs = [((i, 0), (0, 0))] * (i != 0) + [((i, 1), (last, 1))] * (i != last)
        came = send(tied, pairs)
        return jnp.where(section == i, entering_full, came) if i in (0, last) else came

    def fed(t, after):
        tied = entering_full if after is None else lax.optimization_barrier((entering_full, after))[0]
        return jnp.concatenate([piece(i, tied) for i in range(t * per_tick, (t + 1) * per_tick)], axis=0)

    first_cots = jnp.concatenate(
        [
            jnp.concatenate([send(cots, [((i, 1), (last, 1))]), send(cots, [((i, 0), (last, 1))])], axis=1)
            for i in range(per_tick)
        ],
        axis=0,
    )
    first_acts = [entering_full] + [send(entering_full, [((i, 0), (0, 0))]) for i in range(1, per_tick)]
    first_feed = jnp.where(forward, jnp.concatenate(first_acts, axis=0), first_cots)
    x = jnp.concatenate(
        [jnp.where(forward, fwd_in, bwd_in), got[:, :half], jnp.zeros((rows, slots * 2 * rank), bf16)], axis=1
    )

    ring = (
        [((s, 0), (s + 1, 0)) for s in range(last)]
        + [((last, 0), (last, 1))]
        + [((s, 1), (s - 1, 1)) for s in range(1, sections)]
    )
    hist_mine = jnp.zeros((ticks, rows, half), bf16)
    hist_other = jnp.zeros((ticks + 1, rows, half + 2 * rank), bf16)
    feeds = [first_feed, fed(1, None)]
    for tick in range(ticks):
        final = tick + 1 == ticks
        columns = half if final else x.shape[1]
        out, hist_mine, hist_other = pl.pallas_call(
            functools.partial(tick_kernel, tick, ticks, slots, in_scale, out_scale),
            out_shape=(
                shape(rows, columns),
                shape(*hist_mine.shape),
                shape(*hist_other.shape),
            ),
            in_specs=[SMEM, VMEM, VMEM, VMEM, VMEM, VMEM, ANY, ANY],
            out_specs=(VMEM, ANY, ANY),
            scratch_shapes=[
                pltpu.VMEM((rows, half), bf16),
                pltpu.VMEM((2 if final else 1, rows, half + 2 * rank), bf16),
                pltpu.SemaphoreType.DMA((2,)),
            ],
            input_output_aliases={6: 1, 7: 2},
            compiler_params=params(),
            cost_estimate=cost(4 * rows * width * rank, 4 * width * rank),
            name=f"tick{tick}",
        )(where, x, feeds[tick], again_stash, own, other, hist_mine, hist_other)
        if not final:
            x = send(out, ring)
            if tick + 2 < ticks:
                feeds.append(fed(tick + 2, out))
    came = swap(hist_other)
    squeeze_grad, expand_grad, fwd_carry, bwd_carry = pl.pallas_call(
        functools.partial(end_kernel, in_scale, out_scale),
        out_shape=(shape(rank, half), shape(rank, half), shape(rows, half), shape(rows, half)),
        in_specs=[SMEM, VMEM, VMEM, VMEM, VMEM, VMEM],
        out_specs=(VMEM, VMEM, VMEM, VMEM),
        compiler_params=params(),
        cost_estimate=cost(4 * ticks * rows * half * rank, 4 * ticks * rows * half * 2),
        name="finish",
    )(where, hist_mine, hist_other, came, stash, out)

    def averaged(old, late):
        if replicas == 2:
            total = late.astype(f32) + lax.ppermute(late, "dp", [(0, 1), (1, 0)]).astype(f32)
        else:
            total = lax.psum(late, "dp").astype(f32)
        return (old.astype(f32) - STEP_RATE * total / replicas).astype(bf16)

    squeeze_new = averaged(squeeze, squeeze_late[0, 0].T)
    expand_new = averaged(expand, expand_late[0, 0])
    return (
        squeeze_new.T[None],
        expand_new[None],
        squeeze_grad.T[None, None],
        expand_grad[None, None],
        fwd_carry[None, None],
        bwd_carry[None, None],
    )


def solution(mesh):
    placed = (
        P("dp", "pipe", "mp"),
        P("dp", "pipe", "mp"),
        P("pipe", "mp", None),
        P("pipe", None, "mp"),
        P("dp", "pipe", "mp", None),
        P("dp", "pipe", None, "mp"),
        P("dp", "pipe", None, None, "mp"),
        P("dp", "pipe", None, "mp"),
        P("dp", "pipe", None, "mp"),
    )
    return jax.shard_map(
        shards,
        mesh=mesh,
        in_specs=placed,
        out_specs=(
            P("pipe", "mp", None),
            P("pipe", None, "mp"),
            P("dp", "pipe", "mp", None),
            P("dp", "pipe", None, "mp"),
            P("dp", "pipe", None, "mp"),
            P("dp", "pipe", None, "mp"),
        ),
        check_vma=False,
    )
```

```python
import functools
import math

import jax
import jax.numpy as jnp
from jax import lax
from jax.experimental import pallas as pl
from jax.experimental.pallas import tpu as pltpu
from jax.sharding import PartitionSpec as P

BRANCH_SCALE = 0.25
STEP_RATE = 0.5
CHUNK = 512

VMEM = pl.BlockSpec(memory_space=pltpu.VMEM)
SMEM = pl.BlockSpec(memory_space=pltpu.SMEM)
ANY = pl.BlockSpec(memory_space=pl.ANY)
NT = (((1,), (1,)), ((), ()))
TN = (((0,), (0,)), ((), ()))


def dot(a, b, dims=(((1,), (0,)), ((), ()))):
    return lax.dot_general(a, b, dims, preferred_element_type=jnp.float32)


def gelu_and_slope(x):
    c = math.sqrt(2.0 / math.pi)
    t = jnp.tanh(c * (x + 0.044715 * (x * x * x)))
    half = 0.5 * (1.0 + t)
    slope = half + 0.5 * x * (1.0 - t * t) * (c * (1.0 + 3 * 0.044715 * (x * x)))
    return x * half, slope


def split_words(x):
    hi = x.astype(jnp.bfloat16)
    lo = (x - hi.astype(jnp.float32)).astype(jnp.bfloat16)
    return jnp.concatenate([hi, lo], axis=1)


def join_words(words):
    rank = words.shape[1] // 2
    return words[:, :rank].astype(jnp.float32) + words[:, rank:].astype(jnp.float32)


class Place:
    def __init__(self, where):
        self.section, self.role, self.sections = where[0], where[1], where[2]
        self.side = where[3]
        self.forward = self.role == 0
        self.aligned = self.side == self.role
        self.peer = self.section + 1 - 2 * self.side
        pair = jnp.where(self.forward, self.section, self.sections - 1 - self.section)
        self.at_end = pair < 2


class Sizes:
    def __init__(self, ticks, rows, rank, half):
        self.ticks, self.rows, self.rank, self.half = ticks, rows, rank, half
        self.steps = ticks // 2
        self.slots = ticks // 2
        self.width = 2 * half
        self.message = 2 * half + self.slots * 2 * rank
        self.kept = half + 2 * rank
        self.in_scale = 1.0 / math.sqrt(2 * half)
        self.out_scale = BRANCH_SCALE / math.sqrt(rank)


def section_step(size, place, section, tick, x0, x1, again, payload, mine, other, at):
    forward = place.forward
    back = place.sections - 1 - section
    first, second = at + place.role, at + 1 - place.role
    h = (dot(x0, mine[first], NT) + dot(x1, other[first], NT)) * jnp.where(
        forward, size.in_scale, size.out_scale
    )
    for j in range(size.slots):
        ready = jnp.logical_and(back == j, tick >= 2 * j + 1)
        again = jnp.where(ready, join_words(payload[j]), again)
    value, slope = gelu_and_slope(jnp.where(forward, h, again))
    z = jnp.where(forward, value, h * slope).astype(jnp.bfloat16)
    ranks = jnp.concatenate([value.astype(jnp.bfloat16), z], axis=1)
    scale = jnp.where(forward, size.out_scale, size.in_scale)
    y0 = (x0.astype(jnp.float32) + dot(z, mine[second]) * scale).astype(jnp.bfloat16)
    y1 = (x1.astype(jnp.float32) + dot(z, other[second]) * scale).astype(jnp.bfloat16)
    words = split_words(h)
    payload = [jnp.where(jnp.logical_and(forward, back == j), words, payload[j]) for j in range(size.slots)]
    return y0, y1, ranks, payload


def read(size, ref):
    half, span = size.half, 2 * size.rank
    payload = [ref[:, 2 * half + j * span : 2 * half + (j + 1) * span] for j in range(size.slots)]
    return ref[:, :half], ref[:, half : 2 * half], payload


def write(size, ref, y0, y1, payload):
    half, span = size.half, 2 * size.rank
    ref[:, :half] = y0
    ref[:, half : 2 * half] = y1
    for j in range(size.slots):
        ref[:, 2 * half + j * span : 2 * half + (j + 1) * span] = payload[j]


def stash_kernel(size, stash, squeeze, partial):
    ticks, rows, half = stash.shape
    whole = dot(stash[...].reshape(ticks * rows, half), squeeze[...], NT) * size.in_scale
    for t in range(ticks):
        partial[t] = whole[t * rows : (t + 1) * rows]


def keep(size, keep_mine, keep_other, slot, x0, x1, ranks):
    keep_mine[slot] = x0
    keep_other[slot, :, : size.half] = x1
    keep_other[slot, :, size.half :] = ranks


def first_kernel(size, where, x_in, again_own, mine, other, out, hist_mine, hist_other, keep_mine, keep_other, sems):
    place = Place(where)
    x0, x1, payload = read(size, x_in)
    y0, y1, ranks, payload = section_step(
        size, place, place.section, 0, x0, x1, again_own[0], payload, mine, other, 0
    )
    keep(size, keep_mine, keep_other, 0, x0, x1, ranks)
    copies = [
        pltpu.make_async_copy(keep_mine, hist_mine.at[pl.ds(0, 1)], sems.at[0]),
        pltpu.make_async_copy(keep_other, hist_other.at[pl.ds(0, 1)], sems.at[1]),
    ]
    for copy in copies:
        copy.start()
    write(size, out, y0, y1, payload)
    for copy in copies:
        copy.wait()


def second_kernel(size, where, x_in, again_peer, mine, other, out, passed):
    place = Place(where)
    x0, x1, payload = read(size, x_in)
    y0, y1, ranks, sent = section_step(
        size, place, place.peer, 1, x0, x1, again_peer[0], payload, mine, other, 2
    )
    passed[0, :, : size.half] = x0
    passed[1, :, : size.half] = x1
    passed[0, :, size.half :] = ranks
    passed[1, :, size.half :] = ranks
    aligned = place.aligned
    sent = [jnp.where(aligned, sent[j], payload[j]) for j in range(size.slots)]
    write(size, out, jnp.where(aligned, y0, x0), jnp.where(aligned, y1, x1), sent)


def pair_kernel(size, step, where, x_in, feed, again_own, again_peer, mine, other, came, *rest):
    _, _, out, passed, hist_mine, hist_other, keep_mine, keep_other, sems = rest
    half, kept = size.half, size.kept
    place = Place(where)
    aligned = place.aligned
    x0, x1, payload = read(size, x_in)
    x0 = jnp.where(place.at_end, feed[:, :half], x0)
    x1 = jnp.where(place.at_end, feed[:, half:], x1)
    tick = jnp.where(aligned, 2 * step, 2 * step - 1)
    again_peer = again_peer[jnp.where(aligned, step, step - 1)]
    own = again_own[2 * step]
    at_peer = jnp.where(aligned, 0, 2)
    y0, y1, ranks, payload = section_step(
        size, place, jnp.where(aligned, place.section, place.peer), tick, x0, x1,
        jnp.where(aligned, own, again_peer), payload, mine, other, at_peer,
    )
    z0, z1, ranks_b, payload = section_step(
        size, place, jnp.where(aligned, place.peer, place.section), tick + 1, y0, y1,
        jnp.where(aligned, again_peer, own), payload, mine, other, 2 - at_peer,
    )
    keep(
        size, keep_mine, keep_other, 0,
        jnp.where(aligned, x0, y0), jnp.where(aligned, x1, y1), jnp.where(aligned, ranks, ranks_b),
    )
    keep_mine[1] = came[0, :, :half]
    keep_other[1] = came[1, :, :kept]
    odd = jnp.where(aligned, 2 * step - 3 if step > 1 else size.ticks, 2 * step - 1)
    copies = [
        pltpu.make_async_copy(keep_mine.at[pl.ds(0, 1)], hist_mine.at[pl.ds(2 * step, 1)], sems.at[0]),
        pltpu.make_async_copy(keep_other.at[pl.ds(0, 1)], hist_other.at[pl.ds(2 * step, 1)], sems.at[1]),
        pltpu.make_async_copy(keep_mine.at[pl.ds(1, 1)], hist_mine.at[pl.ds(odd, 1)], sems.at[2]),
        pltpu.make_async_copy(keep_other.at[pl.ds(1, 1)], hist_other.at[pl.ds(odd, 1)], sems.at[3]),
    ]
    for copy in copies:
        copy.start()
    ranks_peer = jnp.where(aligned, ranks_b, ranks)
    passed[0, :, :half] = jnp.where(aligned, y0, x0)
    passed[1, :, :half] = jnp.where(aligned, y1, x1)
    passed[0, :, half:kept] = ranks_peer
    passed[1, :, half:kept] = ranks_peer
    if step + 1 == size.steps:
        passed[0, :, kept:] = z0
        passed[1, :, kept:] = z1
    write(size, out, z0, z1, payload)
    for copy in copies:
        copy.wait()


def last_kernel(size, where, x_in, feed, again_peer, mine, other, passed):
    half, kept = size.half, size.kept
    place = Place(where)
    x0, x1, payload = read(size, x_in)
    x0 = jnp.where(place.at_end, feed[:, :half], x0)
    x1 = jnp.where(place.at_end, feed[:, half:], x1)
    y0, y1, ranks, _ = section_step(
        size, place, place.peer, size.ticks - 1, x0, x1, again_peer[size.steps - 1], payload, mine, other, 2
    )
    passed[0, :, :half] = x0
    passed[1, :, :half] = x1
    passed[0, :, half:kept] = ranks
    passed[1, :, half:kept] = ranks
    passed[0, :, kept:] = y0
    passed[1, :, kept:] = y1


def end_kernel(size, where, mine, sent, got, late, late_got, last, last_got, stash, squeeze_grad, expand_grad, fwd, bwd):
    ticks, half, kept, rank = size.ticks, size.half, size.kept, size.rank
    place = Place(where)
    forward = place.forward

    def block(role, t, cols, part=0):
        aligned = place.side == role
        here = place.role == role

        def pick(own, other):
            return jnp.where(here, own, other)

        def hist():
            own = mine[t, :, cols] if part == 0 else sent[t, :, cols]
            return pick(own, got[t, :, cols])

        if t == ticks - 3:
            return jnp.where(aligned, pick(late[part, :, cols], late_got[:, cols]), hist())
        if t == ticks - 1:
            return jnp.where(
                aligned,
                pick(last[part, :, cols], last_got[:, cols]),
                pick(late[part, :, cols], late_got[:, cols]),
            )
        return hist()

    lag = 2 * (place.sections - 1 - place.section) + 1
    ranks = jnp.concatenate([block(1, t, slice(half, kept), 1) for t in range(ticks)], axis=0)
    regated, hidden_grad = ranks[:, :rank], ranks[:, rank:]
    for lo in range(0, half, CHUNK):
        cols = slice(lo, min(lo + CHUNK, half))
        a = [block(0, t, cols) for t in range(ticks - 1)]
        u = []
        for t in range(ticks):
            at = stash[t, :, cols]
            for j in range((t + 1) // 2):
                at = jnp.where(lag == 2 * j + 1, a[t - 2 * j - 1], at)
            u.append(at)
        u = jnp.concatenate(u, axis=0)
        g = jnp.concatenate([block(1, t, cols) for t in range(ticks)], axis=0)
        squeeze_grad[:, cols] = (dot(hidden_grad, u, TN) * size.in_scale).astype(jnp.bfloat16)
        expand_grad[:, cols] = (dot(regated, g, TN) * size.out_scale).astype(jnp.bfloat16)

    def carry(role):
        here = place.role == role
        early = jnp.where(here, late[0, :, kept:], late_got[:, kept:])
        final = jnp.where(here, last[0, :, kept:], last_got[:, kept:])
        return jnp.where(place.side == role, final, early)

    fwd[...] = carry(0)
    bwd[...] = carry(1)


def params():
    return pltpu.CompilerParams(vmem_limit_bytes=24 * 1024 * 1024)


def shape(*dims, dtype=jnp.bfloat16):
    return jax.ShapeDtypeStruct(dims, dtype)


def shards(
    activations,
    cotangent,
    squeeze_old,
    expand_old,
    squeeze_late,
    expand_late,
    stash_inputs,
    forward_in,
    backward_in,
):
    sections = lax.axis_size("pipe")
    replicas = lax.axis_size("dp")
    section = lax.axis_index("pipe")
    role = lax.axis_index("mp")
    half, rank = squeeze_old.shape[1], squeeze_old.shape[2]
    ticks, rows = stash_inputs.shape[2], stash_inputs.shape[3]
    size = Sizes(ticks, rows, rank, half)
    bf16, f32 = jnp.bfloat16, jnp.float32
    everyone = range(sections)

    def send(x, pairs):
        return lax.ppermute(x, ("pipe", "mp"), [(a * 2 + b, c * 2 + d) for (a, b), (c, d) in pairs])

    def swap(x):
        return lax.ppermute(x, "mp", [(0, 1), (1, 0)])

    def to_peer(x, senders):
        return send(x, [((s, c), (s ^ 1, c)) for s, c in senders])

    def tied(x, *others):
        return lax.optimization_barrier((x, *others))[0]

    def call(body, name, outs, in_specs, out_specs, scratch=(), aliases=None):
        return pl.pallas_call(
            functools.partial(body, size),
            out_shape=outs,
            in_specs=in_specs,
            out_specs=out_specs,
            scratch_shapes=list(scratch),
            input_output_aliases=aliases or {},
            compiler_params=params(),
            cost_estimate=pl.CostEstimate(
                flops=8 * rows * size.width * rank, bytes_accessed=8 * size.width * rank, transcendentals=0
            ),
            name=name,
        )

    side = section % 2
    where = jnp.stack([section, role, jnp.int32(sections), side]).astype(jnp.int32)
    forward = role == 0
    squeeze, expand = squeeze_old[0].T, expand_old[0]
    stash = stash_inputs[0, 0]
    fwd_in, bwd_in = forward_in[0, 0], backward_in[0, 0]
    acts, cots = activations[0], cotangent[0]
    both = [(s, c) for s in everyone for c in (0, 1)]

    squeeze_peer, expand_peer = to_peer(squeeze, both), to_peer(expand, both)
    own = jnp.stack([squeeze, expand])
    other = swap(own)
    mine_all = jnp.concatenate([own, squeeze_peer[None], expand_peer[None]], axis=0)
    other_all = jnp.concatenate([other, swap(squeeze_peer)[None], swap(expand_peer)[None]], axis=0)

    partial = call(
        stash_kernel, "stashed", shape(ticks, rows, rank, dtype=f32), [VMEM, VMEM], VMEM
    )(stash, squeeze)
    again_own = partial + swap(partial)
    again_peer = to_peer(again_own[1::2], [(s, 1) for s in everyone])

    entering_full = jnp.concatenate(
        [jnp.where(forward, acts, cots), swap(jnp.where(forward, cots, acts))], axis=1
    )
    per_tick = rows // acts.shape[0]

    def fed(step):
        pieces = []
        for m in range(per_tick):
            blocks = [b for b in (2 * step, 2 * step - 1) if 0 <= b < ticks]
            moves = [((b * per_tick + m, 0), (b % 2, 0)) for b in blocks]
            moves += [((b * per_tick + m, 1), (sections - 1 - b % 2, 1)) for b in blocks]
            came = send(entering_full, [(a, b) for a, b in moves if a != b])
            for a, b in moves:
                if a == b:
                    here = jnp.logical_and(section == a[0], role == a[1])
                    came = jnp.where(here, entering_full, came)
            pieces.append(came)
        return jnp.concatenate(pieces, axis=0)

    first_cots, first_acts = [], []
    for i in range(per_tick):
        halves = [send(cots, [((i, c), (sections - 1, 1))]) for c in (1, 0)]
        first_cots.append(jnp.concatenate(halves, axis=1))
        first_acts.append(entering_full if i == 0 else send(entering_full, [((i, 0), (0, 0))]))
    first_feed = jnp.where(forward, jnp.concatenate(first_acts, axis=0), jnp.concatenate(first_cots, axis=0))
    first_end = section == jnp.where(forward, 0, sections - 1)
    x = jnp.concatenate([jnp.where(forward, fwd_in, bwd_in), swap(jnp.where(forward, bwd_in, fwd_in))], axis=1)
    x = jnp.concatenate([jnp.where(first_end, first_feed, x), jnp.zeros((rows, size.message - size.width), bf16)], axis=1)
    feeds = {1: fed(1), 2: fed(2)}

    hist_shapes = (shape(ticks + 1, rows, half), shape(ticks + 1, rows, size.kept))

    def scratch(n):
        return (
            pltpu.VMEM((n, rows, half), bf16),
            pltpu.VMEM((n, rows, size.kept), bf16),
            pltpu.SemaphoreType.DMA((2 * n,)),
        )

    def averaged(old, late):
        if replicas == 2:
            total = late.astype(f32) + lax.ppermute(late, "dp", [(0, 1), (1, 0)]).astype(f32)
        else:
            total = lax.psum(late, "dp").astype(f32)
        return (old.astype(f32) - STEP_RATE * total / replicas).astype(bf16)

    squeeze_new = averaged(squeeze, squeeze_late[0, 0].T)
    expand_new = averaged(expand, expand_late[0, 0])

    ring = (
        [((s, 0), (s + 2, 0)) for s in range(sections - 2)]
        + [((sections - 2, 0), (sections - 1, 1)), ((sections - 1, 0), (sections - 2, 1))]
        + [((s, 1), (s - 2, 1)) for s in range(2, sections)]
    )
    aligned = [(s, s % 2) for s in everyone]
    late_ones = [(s, 1 - s % 2) for s in everyone]

    x, hist_mine, hist_other = call(
        first_kernel, "first", (shape(rows, size.message), *hist_shapes),
        [SMEM, VMEM, VMEM, VMEM, VMEM], (VMEM, ANY, ANY), scratch(1),
    )(where, x, again_own, own, other)
    x, passed = call(
        second_kernel, "second", (shape(rows, size.message), shape(2, rows, size.kept)),
        [SMEM, VMEM, VMEM, VMEM, VMEM], (VMEM, VMEM),
    )(where, tied(x, feeds[1], feeds[2]), again_peer, mine_all, other_all)
    came = to_peer(passed, aligned)
    x = send(x, ring)
    for step in range(1, size.steps):
        final = step + 1 == size.steps
        if step == 2:
            x = tied(x, squeeze_new)
        if step == 3:
            x = tied(x, expand_new)
        x, passed, hist_mine, hist_other = call(
            lambda size, *refs, step=step: pair_kernel(size, step, *refs), f"pair{step}",
            (
                shape(rows, size.message),
                shape(2, rows, size.kept + (half if final else 0)),
                *hist_shapes,
            ),
            [SMEM, VMEM, VMEM, VMEM, VMEM, VMEM, VMEM, VMEM, ANY, ANY], (VMEM, VMEM, ANY, ANY),
            scratch(2), {8: 2, 9: 3},
        )(where, x, feeds[step], again_own, again_peer, mine_all, other_all, came, hist_mine, hist_other)
        if step + 2 not in feeds and step + 2 <= size.steps:
            feeds[step + 2] = fed(step + 2)
        x = send(x, ring)
        came = to_peer(passed, both)
    hist_got = swap(hist_other)
    late, late_got = came, swap(came[1])
    passed = call(
        last_kernel, "last", shape(2, rows, size.kept + half),
        [SMEM, VMEM, VMEM, VMEM, VMEM, VMEM], VMEM,
    )(where, x, feeds[size.steps], again_peer, mine_all, other_all)
    last = to_peer(passed, late_ones)
    last_got = swap(last[1])
    squeeze_grad, expand_grad, fwd_carry, bwd_carry = call(
        end_kernel, "finish",
        (shape(rank, half), shape(rank, half), shape(rows, half), shape(rows, half)),
        [SMEM] + [VMEM] * 8, (VMEM,) * 4,
    )(where, hist_mine, hist_other, hist_got, late, late_got, last, last_got, stash)
    return (
        squeeze_new.T[None],
        expand_new[None],
        squeeze_grad.T[None, None],
        expand_grad[None, None],
        fwd_carry[None, None],
        bwd_carry[None, None],
    )


def solution(mesh):
    placed = (
        P("dp", "pipe", "mp"),
        P("dp", "pipe", "mp"),
        P("pipe", "mp", None),
        P("pipe", None, "mp"),
        P("dp", "pipe", "mp", None),
        P("dp", "pipe", None, "mp"),
        P("dp", "pipe", None, None, "mp"),
        P("dp", "pipe", None, "mp"),
        P("dp", "pipe", None, "mp"),
    )
    return jax.shard_map(
        shards,
        mesh=mesh,
        in_specs=placed,
        out_specs=(
            P("pipe", "mp", None),
            P("pipe", None, "mp"),
            P("dp", "pipe", "mp", None),
            P("dp", "pipe", None, "mp"),
            P("dp", "pipe", None, "mp"),
            P("dp", "pipe", None, "mp"),
        ),
        check_vma=False,
    )
```

```python
import functools
import math

import jax
import jax.numpy as jnp
from jax import lax
from jax.experimental import pallas as pl
from jax.experimental.pallas import tpu as pltpu
from jax.sharding import PartitionSpec as P

BRANCH_SCALE = 0.25
STEP_RATE = 0.5
CHUNK = 512

VMEM = pl.BlockSpec(memory_space=pltpu.VMEM)
SMEM = pl.BlockSpec(memory_space=pltpu.SMEM)
ANY = pl.BlockSpec(memory_space=pl.ANY)
NT = (((1,), (1,)), ((), ()))
TN = (((0,), (0,)), ((), ()))


def dot(a, b, dims=(((1,), (0,)), ((), ()))):
    return lax.dot_general(a, b, dims, preferred_element_type=jnp.float32)


def gelu_and_slope(x):
    c = math.sqrt(2.0 / math.pi)
    t = jnp.tanh(c * (x + 0.044715 * (x * x * x)))
    half = 0.5 * (1.0 + t)
    slope = half + 0.5 * x * (1.0 - t * t) * (c * (1.0 + 3 * 0.044715 * (x * x)))
    return x * half, slope


def split_words(x):
    hi = x.astype(jnp.bfloat16)
    lo = (x - hi.astype(jnp.float32)).astype(jnp.bfloat16)
    return jnp.concatenate([hi, lo], axis=1)


def join_words(words):
    rank = words.shape[1] // 2
    return words[:, :rank].astype(jnp.float32) + words[:, rank:].astype(jnp.float32)


class Place:
    def __init__(self, where):
        self.section, self.role, self.sections = where[0], where[1], where[2]
        self.side = where[3]
        self.forward = self.role == 0
        self.aligned = self.side == self.role
        self.peer = self.section + 1 - 2 * self.side
        pair = jnp.where(self.forward, self.section, self.sections - 1 - self.section)
        self.at_end = pair < 2


class Sizes:
    def __init__(self, ticks, rows, rank, half):
        self.ticks, self.rows, self.rank, self.half = ticks, rows, rank, half
        self.steps = ticks // 2
        self.slots = ticks // 2
        self.width = 2 * half
        self.message = 2 * half + self.slots * 2 * rank
        self.kept = half + 2 * rank
        self.in_scale = 1.0 / math.sqrt(2 * half)
        self.out_scale = BRANCH_SCALE / math.sqrt(rank)


def section_step(size, place, section, tick, x0, x1, again, payload, mine, other, at):
    forward = place.forward
    back = place.sections - 1 - section
    first, second = at + place.role, at + 1 - place.role
    h = (dot(x0, mine[first], NT) + dot(x1, other[first], NT)) * jnp.where(
        forward, size.in_scale, size.out_scale
    )
    for j in range(size.slots):
        ready = jnp.logical_and(back == j, tick >= 2 * j + 1)
        again = jnp.where(ready, join_words(payload[j]), again)
    value, slope = gelu_and_slope(jnp.where(forward, h, again))
    z = jnp.where(forward, value, h * slope).astype(jnp.bfloat16)
    ranks = jnp.concatenate([value.astype(jnp.bfloat16), z], axis=1)
    scale = jnp.where(forward, size.out_scale, size.in_scale)
    y0 = (x0.astype(jnp.float32) + dot(z, mine[second]) * scale).astype(jnp.bfloat16)
    y1 = (x1.astype(jnp.float32) + dot(z, other[second]) * scale).astype(jnp.bfloat16)
    words = split_words(h)
    payload = [jnp.where(jnp.logical_and(forward, back == j), words, payload[j]) for j in range(size.slots)]
    return y0, y1, ranks, payload


def read(size, ref):
    half, span = size.half, 2 * size.rank
    payload = [ref[:, 2 * half + j * span : 2 * half + (j + 1) * span] for j in range(size.slots)]
    return ref[:, :half], ref[:, half : 2 * half], payload


def write(size, ref, y0, y1, payload):
    half, span = size.half, 2 * size.rank
    ref[:, :half] = y0
    ref[:, half : 2 * half] = y1
    for j in range(size.slots):
        ref[:, 2 * half + j * span : 2 * half + (j + 1) * span] = payload[j]


def stash_kernel(size, stash, squeeze, partial):
    ticks, rows, half = stash.shape
    whole = dot(stash[...].reshape(ticks * rows, half), squeeze[...], NT) * size.in_scale
    for t in range(ticks):
        partial[t] = whole[t * rows : (t + 1) * rows]


def keep(size, keep_mine, keep_other, slot, x0, x1, ranks):
    keep_mine[slot] = x0
    keep_other[slot, :, : size.half] = x1
    keep_other[slot, :, size.half :] = ranks


def first_kernel(size, where, x_in, again_own, mine, other, out, hist_mine, hist_other, keep_mine, keep_other, sems):
    place = Place(where)
    x0, x1, payload = read(size, x_in)
    y0, y1, ranks, payload = section_step(
        size, place, place.section, 0, x0, x1, again_own[0], payload, mine, other, 0
    )
    keep(size, keep_mine, keep_other, 0, x0, x1, ranks)
    copies = [
        pltpu.make_async_copy(keep_mine, hist_mine.at[pl.ds(0, 1)], sems.at[0]),
        pltpu.make_async_copy(keep_other, hist_other.at[pl.ds(0, 1)], sems.at[1]),
    ]
    for copy in copies:
        copy.start()
    write(size, out, y0, y1, payload)
    for copy in copies:
        copy.wait()


def second_kernel(size, where, x_in, again_peer, mine, other, out, passed):
    place = Place(where)
    x0, x1, payload = read(size, x_in)
    y0, y1, ranks, sent = section_step(
        size, place, place.peer, 1, x0, x1, again_peer[0], payload, mine, other, 2
    )
    passed[0, :, : size.half] = x0
    passed[1, :, : size.half] = x1
    passed[0, :, size.half :] = ranks
    passed[1, :, size.half :] = ranks
    aligned = place.aligned
    sent = [jnp.where(aligned, sent[j], payload[j]) for j in range(size.slots)]
    write(size, out, jnp.where(aligned, y0, x0), jnp.where(aligned, y1, x1), sent)


def pair_kernel(size, step, where, x_in, feed, again_own, again_peer, mine, other, came, *rest):
    _, _, out, passed, hist_mine, hist_other, keep_mine, keep_other, sems = rest
    half, kept = size.half, size.kept
    place = Place(where)
    aligned = place.aligned
    x0, x1, payload = read(size, x_in)
    x0 = jnp.where(place.at_end, feed[:, :half], x0)
    x1 = jnp.where(place.at_end, feed[:, half:], x1)
    tick = jnp.where(aligned, 2 * step, 2 * step - 1)
    again_peer = again_peer[jnp.where(aligned, step, step - 1)]
    own = again_own[2 * step]
    at_peer = jnp.where(aligned, 0, 2)
    y0, y1, ranks, payload = section_step(
        size, place, jnp.where(aligned, place.section, place.peer), tick, x0, x1,
        jnp.where(aligned, own, again_peer), payload, mine, other, at_peer,
    )
    z0, z1, ranks_b, payload = section_step(
        size, place, jnp.where(aligned, place.peer, place.section), tick + 1, y0, y1,
        jnp.where(aligned, again_peer, own), payload, mine, other, 2 - at_peer,
    )
    keep(
        size, keep_mine, keep_other, 0,
        jnp.where(aligned, x0, y0), jnp.where(aligned, x1, y1), jnp.where(aligned, ranks, ranks_b),
    )
    keep_mine[1] = came[0, :, :half]
    keep_other[1] = came[1, :, :kept]
    odd = jnp.where(aligned, 2 * step - 3 if step > 1 else size.ticks, 2 * step - 1)
    copies = [
        pltpu.make_async_copy(keep_mine.at[pl.ds(0, 1)], hist_mine.at[pl.ds(2 * step, 1)], sems.at[0]),
        pltpu.make_async_copy(keep_other.at[pl.ds(0, 1)], hist_other.at[pl.ds(2 * step, 1)], sems.at[1]),
        pltpu.make_async_copy(keep_mine.at[pl.ds(1, 1)], hist_mine.at[pl.ds(odd, 1)], sems.at[2]),
        pltpu.make_async_copy(keep_other.at[pl.ds(1, 1)], hist_other.at[pl.ds(odd, 1)], sems.at[3]),
    ]
    for copy in copies:
        copy.start()
    ranks_peer = jnp.where(aligned, ranks_b, ranks)
    passed[0, :, :half] = jnp.where(aligned, y0, x0)
    passed[1, :, :half] = jnp.where(aligned, y1, x1)
    passed[0, :, half:kept] = ranks_peer
    passed[1, :, half:kept] = ranks_peer
    if step + 1 == size.steps:
        passed[0, :, kept:] = z0
        passed[1, :, kept:] = z1
    write(size, out, z0, z1, payload)
    for copy in copies:
        copy.wait()


def last_kernel(size, where, x_in, feed, again_own, mine, other, last_mine, last_other):
    half, kept = size.half, size.kept
    place = Place(where)
    x0, x1, payload = read(size, x_in)
    x0 = jnp.where(place.at_end, feed[:, :half], x0)
    x1 = jnp.where(place.at_end, feed[:, half:], x1)
    tick = size.ticks - 1
    y0, y1, ranks, _ = section_step(
        size, place, place.section, tick, x0, x1, again_own[tick], payload, mine, other, 0
    )
    for ref, x, y in ((last_mine, x0, y0), (last_other, x1, y1)):
        ref[:, :half] = x
        ref[:, half:kept] = ranks
        ref[:, kept:] = y


def end_kernel(size, where, mine, sent, got, late, late_got, last_mine, last_other, last_got, stash, *outs):
    squeeze_grad, expand_grad, fwd, bwd = outs
    ticks, half, kept, rank = size.ticks, size.half, size.kept, size.rank
    place = Place(where)
    forward = place.forward

    def block(role, t, cols, part=0):
        aligned = place.side == role
        here = place.role == role

        def pick(own, other):
            return jnp.where(here, own, other)

        def hist():
            own = mine[t, :, cols] if part == 0 else sent[t, :, cols]
            return pick(own, got[t, :, cols])

        if t == ticks - 3:
            return jnp.where(aligned, pick(late[part, :, cols], late_got[:, cols]), hist())
        if t == ticks - 1:
            return jnp.where(
                aligned,
                pick((last_mine, last_other)[part][:, cols], last_got[:, cols]),
                pick(late[part, :, cols], late_got[:, cols]),
            )
        return hist()

    lag = 2 * (place.sections - 1 - place.section) + 1
    ranks = jnp.concatenate([block(1, t, slice(half, kept), 1) for t in range(ticks)], axis=0)
    regated, hidden_grad = ranks[:, :rank], ranks[:, rank:]
    for lo in range(0, half, CHUNK):
        cols = slice(lo, min(lo + CHUNK, half))
        a = [block(0, t, cols) for t in range(ticks - 1)]
        u = []
        for t in range(ticks):
            at = stash[t, :, cols]
            for j in range((t + 1) // 2):
                at = jnp.where(lag == 2 * j + 1, a[t - 2 * j - 1], at)
            u.append(at)
        u = jnp.concatenate(u, axis=0)
        g = jnp.concatenate([block(1, t, cols) for t in range(ticks)], axis=0)
        squeeze_grad[:, cols] = (dot(hidden_grad, u, TN) * size.in_scale).astype(jnp.bfloat16)
        expand_grad[:, cols] = (dot(regated, g, TN) * size.out_scale).astype(jnp.bfloat16)

    def carry(role):
        here = place.role == role
        early = jnp.where(here, late[0, :, kept:], late_got[:, kept:])
        final = jnp.where(here, last_mine[:, kept:], last_got[:, kept:])
        return jnp.where(place.side == role, final, early)

    fwd[...] = carry(0)
    bwd[...] = carry(1)


def params():
    return pltpu.CompilerParams(vmem_limit_bytes=24 * 1024 * 1024)


def shape(*dims, dtype=jnp.bfloat16):
    return jax.ShapeDtypeStruct(dims, dtype)


def shards(
    activations,
    cotangent,
    squeeze_old,
    expand_old,
    squeeze_late,
    expand_late,
    stash_inputs,
    forward_in,
    backward_in,
):
    sections = lax.axis_size("pipe")
    replicas = lax.axis_size("dp")
    section = lax.axis_index("pipe")
    role = lax.axis_index("mp")
    half, rank = squeeze_old.shape[1], squeeze_old.shape[2]
    ticks, rows = stash_inputs.shape[2], stash_inputs.shape[3]
    size = Sizes(ticks, rows, rank, half)
    bf16, f32 = jnp.bfloat16, jnp.float32
    everyone = range(sections)

    def send(x, pairs):
        return lax.ppermute(x, ("pipe", "mp"), [(a * 2 + b, c * 2 + d) for (a, b), (c, d) in pairs])

    def swap(x):
        return lax.ppermute(x, "mp", [(0, 1), (1, 0)])

    def to_peer(x, senders):
        return send(x, [((s, c), (s ^ 1, c)) for s, c in senders])

    def tied(x, *others):
        return lax.optimization_barrier((x, *others))[0]

    def call(body, name, outs, in_specs, out_specs, scratch=(), aliases=None):
        return pl.pallas_call(
            functools.partial(body, size),
            out_shape=outs,
            in_specs=in_specs,
            out_specs=out_specs,
            scratch_shapes=list(scratch),
            input_output_aliases=aliases or {},
            compiler_params=params(),
            cost_estimate=pl.CostEstimate(
                flops=8 * rows * size.width * rank, bytes_accessed=8 * size.width * rank, transcendentals=0
            ),
            name=name,
        )

    side = section % 2
    where = jnp.stack([section, role, jnp.int32(sections), side]).astype(jnp.int32)
    forward = role == 0
    squeeze, expand = squeeze_old[0].T, expand_old[0]
    stash = stash_inputs[0, 0]
    fwd_in, bwd_in = forward_in[0, 0], backward_in[0, 0]
    acts, cots = activations[0], cotangent[0]
    both = [(s, c) for s in everyone for c in (0, 1)]

    squeeze_peer = to_peer(squeeze, both)
    expand_peer = to_peer(tied(expand, squeeze_peer), both)
    own = jnp.stack([squeeze, expand])
    other = swap(own)
    squeeze_peer_other = swap(squeeze_peer)

    partial = call(
        stash_kernel, "stashed", shape(ticks, rows, rank, dtype=f32), [VMEM, VMEM], VMEM
    )(stash, squeeze)
    again_own = partial + swap(partial)
    again_peer = to_peer(again_own[1::2], [(s, 1) for s in everyone])

    entering_full = jnp.concatenate(
        [jnp.where(forward, acts, cots), swap(jnp.where(forward, cots, acts))], axis=1
    )
    per_tick = rows // acts.shape[0]

    def fed(step, *after):
        pieces = []
        entering_now = tied(entering_full, *after) if after else entering_full
        for m in range(per_tick):
            moves = []
            for b in (2 * step, 2 * step - 1):
                if 0 <= b < ticks:
                    to = b % 2 if step < size.steps else 0
                    moves += [((b * per_tick + m, 0), (to, 0)), ((b * per_tick + m, 1), (sections - 1 - to, 1))]
            came = send(entering_now, [(a, b) for a, b in moves if a != b])
            for a, b in moves:
                if a == b:
                    here = jnp.logical_and(section == a[0], role == a[1])
                    came = jnp.where(here, entering_full, came)
            pieces.append(came)
        return jnp.concatenate(pieces, axis=0)

    feeds = [fed(0)]
    for step in range(1, size.steps + 1):
        feeds.append(fed(step, *(feeds[:1] if step < 3 else feeds[step - 2 : step])))
    first_end = section == jnp.where(forward, 0, sections - 1)
    x = jnp.concatenate([jnp.where(forward, fwd_in, bwd_in), swap(jnp.where(forward, bwd_in, fwd_in))], axis=1)
    x = jnp.concatenate([jnp.where(first_end, feeds[0], x), jnp.zeros((rows, size.message - size.width), bf16)], axis=1)

    hist_shapes = (shape(ticks + 1, rows, half), shape(ticks + 1, rows, size.kept))

    def scratch(n):
        return (
            pltpu.VMEM((n, rows, half), bf16),
            pltpu.VMEM((n, rows, size.kept), bf16),
            pltpu.SemaphoreType.DMA((2 * n,)),
        )

    def averaged(old, late):
        if replicas == 2:
            came = lax.ppermute(late, "dp", [(0, 1), (1, 0)])
            total = late.astype(f32) + came.astype(f32)
        else:
            came = lax.psum(late, "dp")
            total = came.astype(f32)
        return (old.astype(f32) - STEP_RATE * total / replicas).astype(bf16), came

    squeeze_new, came = averaged(squeeze, squeeze_late[0, 0].T)
    expand_new, _ = averaged(expand, tied(expand_late[0, 0], came))

    ring = (
        [((s, 0), (s + 2, 0)) for s in range(sections - 2)]
        + [((sections - 2, 0), (sections - 1, 1)), ((sections - 1, 0), (sections - 2, 1))]
        + [((s, 1), (s - 2, 1)) for s in range(2, sections)]
    )
    aligned = [(s, s % 2) for s in everyone]
    ring_last = (
        [((s, 0), (s + 1, 0)) for s in range(1, sections - 1, 2)]
        + [((sections - 1, 0), (sections - 1, 1))]
        + [((s, 1), (s - 1, 1)) for s in range(2, sections, 2)]
    )

    x, hist_mine, hist_other = call(
        first_kernel, "first", (shape(rows, size.message), *hist_shapes),
        [SMEM, VMEM, VMEM, VMEM, VMEM], (VMEM, ANY, ANY), scratch(1),
    )(where, x, again_own, own, other)
    expand_peer_other = swap(tied(expand_peer, x))
    mine_all = jnp.concatenate([own, squeeze_peer[None], expand_peer[None]], axis=0)
    other_all = jnp.concatenate([other, squeeze_peer_other[None], expand_peer_other[None]], axis=0)
    x, passed = call(
        second_kernel, "second", (shape(rows, size.message), shape(2, rows, size.kept)),
        [SMEM, VMEM, VMEM, VMEM, VMEM], (VMEM, VMEM),
    )(where, tied(x, *feeds[1:]), again_peer, mine_all, other_all)
    came = to_peer(passed, aligned)
    x = send(x, ring)
    for step in range(1, size.steps):
        final = step + 1 == size.steps
        if step == 1:
            x = tied(x, squeeze_new)
        if step == 2:
            x = tied(x, expand_new)
        x, passed, hist_mine, hist_other = call(
            lambda size, *refs, step=step: pair_kernel(size, step, *refs), f"pair{step}",
            (
                shape(rows, size.message),
                shape(2, rows, size.kept + (half if final else 0)),
                *hist_shapes,
            ),
            [SMEM, VMEM, VMEM, VMEM, VMEM, VMEM, VMEM, VMEM, ANY, ANY], (VMEM, VMEM, ANY, ANY),
            scratch(2), {8: 2, 9: 3},
        )(where, x, feeds[step], again_own, again_peer, mine_all, other_all, came, hist_mine, hist_other)
        x = send(x, ring_last if final else ring)
        came = to_peer(passed, both)
    hist_got = swap(hist_other)
    late, late_got = came, swap(came[1])
    last_mine, last_other = call(
        last_kernel, "last", (shape(rows, size.kept + half), shape(rows, size.kept + half)),
        [SMEM, VMEM, VMEM, VMEM, VMEM, VMEM], (VMEM, VMEM),
    )(where, x, feeds[size.steps], again_own, own, other)
    last_got = swap(last_other)
    squeeze_grad, expand_grad, fwd_carry, bwd_carry = call(
        end_kernel, "finish",
        (shape(rank, half), shape(rank, half), shape(rows, half), shape(rows, half)),
        [SMEM] + [VMEM] * 9, (VMEM,) * 4,
    )(where, hist_mine, hist_other, hist_got, late, late_got, last_mine, last_other, last_got, stash)
    return (
        squeeze_new.T[None],
        expand_new[None],
        squeeze_grad.T[None, None],
        expand_grad[None, None],
        fwd_carry[None, None],
        bwd_carry[None, None],
    )


def solution(mesh):
    placed = (
        P("dp", "pipe", "mp"),
        P("dp", "pipe", "mp"),
        P("pipe", "mp", None),
        P("pipe", None, "mp"),
        P("dp", "pipe", "mp", None),
        P("dp", "pipe", None, "mp"),
        P("dp", "pipe", None, None, "mp"),
        P("dp", "pipe", None, "mp"),
        P("dp", "pipe", None, "mp"),
    )
    return jax.shard_map(
        shards,
        mesh=mesh,
        in_specs=placed,
        out_specs=(
            P("pipe", "mp", None),
            P("pipe", None, "mp"),
            P("dp", "pipe", "mp", None),
            P("dp", "pipe", None, "mp"),
            P("dp", "pipe", None, "mp"),
            P("dp", "pipe", None, "mp"),
        ),
        check_vma=False,
    )
```

```python
import functools
import math

import jax
import jax.numpy as jnp
from jax import lax
from jax.experimental import pallas as pl
from jax.experimental.pallas import tpu as pltpu
from jax.sharding import PartitionSpec as P

BRANCH_SCALE = 0.25
STEP_RATE = 0.5
CHUNK = 512

VMEM = pl.BlockSpec(memory_space=pltpu.VMEM)
SMEM = pl.BlockSpec(memory_space=pltpu.SMEM)
ANY = pl.BlockSpec(memory_space=pl.ANY)
NT = (((1,), (1,)), ((), ()))
TN = (((0,), (0,)), ((), ()))


def dot(a, b, dims=(((1,), (0,)), ((), ()))):
    return lax.dot_general(a, b, dims, preferred_element_type=jnp.float32)


def gelu_and_slope(x):
    c = math.sqrt(2.0 / math.pi)
    t = jnp.tanh(c * (x + 0.044715 * (x * x * x)))
    half = 0.5 * (1.0 + t)
    slope = half + 0.5 * x * (1.0 - t * t) * (c * (1.0 + 3 * 0.044715 * (x * x)))
    return x * half, slope


def split_words(x):
    hi = x.astype(jnp.bfloat16)
    lo = (x - hi.astype(jnp.float32)).astype(jnp.bfloat16)
    return jnp.concatenate([hi, lo], axis=1)


def join_words(words):
    rank = words.shape[1] // 2
    return words[:, :rank].astype(jnp.float32) + words[:, rank:].astype(jnp.float32)


class Place:
    def __init__(self, where):
        self.section, self.role, self.sections = where[0], where[1], where[2]
        self.side = where[3]
        self.forward = self.role == 0
        self.aligned = self.side == self.role
        self.peer = self.section + 1 - 2 * self.side
        pair = jnp.where(self.forward, self.section, self.sections - 1 - self.section)
        self.at_end = pair < 2


class Sizes:
    def __init__(self, ticks, rows, rank, half):
        self.ticks, self.rows, self.rank, self.half = ticks, rows, rank, half
        self.steps = ticks // 2
        self.slots = ticks // 2
        self.width = 2 * half
        self.message = 2 * half + self.slots * 2 * rank
        self.kept = half + 2 * rank
        self.in_scale = 1.0 / math.sqrt(2 * half)
        self.out_scale = BRANCH_SCALE / math.sqrt(rank)


def section_step(size, place, section, tick, x0, x1, again, payload, mine, other, at):
    forward = place.forward
    back = place.sections - 1 - section
    first, second = at + place.role, at + 1 - place.role
    h = (dot(x0, mine[first], NT) + dot(x1, other[first], NT)) * jnp.where(
        forward, size.in_scale, size.out_scale
    )
    for j in range(size.slots):
        ready = jnp.logical_and(back == j, tick >= 2 * j + 1)
        again = jnp.where(ready, join_words(payload[j]), again)
    value, slope = gelu_and_slope(jnp.where(forward, h, again))
    z = jnp.where(forward, value, h * slope).astype(jnp.bfloat16)
    ranks = jnp.concatenate([value.astype(jnp.bfloat16), z], axis=1)
    scale = jnp.where(forward, size.out_scale, size.in_scale)
    y0 = (x0.astype(jnp.float32) + dot(z, mine[second]) * scale).astype(jnp.bfloat16)
    y1 = (x1.astype(jnp.float32) + dot(z, other[second]) * scale).astype(jnp.bfloat16)
    words = split_words(h)
    payload = [jnp.where(jnp.logical_and(forward, back == j), words, payload[j]) for j in range(size.slots)]
    return y0, y1, ranks, payload


def read(size, ref):
    half, span = size.half, 2 * size.rank
    payload = [ref[:, 2 * half + j * span : 2 * half + (j + 1) * span] for j in range(size.slots)]
    return ref[:, :half], ref[:, half : 2 * half], payload


def write(size, ref, y0, y1, payload):
    half, span = size.half, 2 * size.rank
    ref[:, :half] = y0
    ref[:, half : 2 * half] = y1
    for j in range(size.slots):
        ref[:, 2 * half + j * span : 2 * half + (j + 1) * span] = payload[j]


def stash_kernel(size, stash, squeeze, partial):
    ticks, rows, half = stash.shape
    whole = dot(stash[...].reshape(ticks * rows, half), squeeze[...], NT) * size.in_scale
    for t in range(ticks):
        partial[t] = whole[t * rows : (t + 1) * rows]


def keep(size, keep_mine, keep_other, x0, x1, ranks):
    keep_mine[0] = x0
    keep_other[0, :, : size.half] = x1
    keep_other[0, :, size.half :] = ranks


def keep_passed(size, ref, x0, x1, ranks):
    half, kept = size.half, size.kept
    for part, x in enumerate((x0, x1)):
        ref[part, 0, :, :half] = x
        ref[part, 0, :, half:kept] = ranks


def first_kernel(size, where, x_in, again_own, mine, other, out, hist_mine, hist_other, keep_mine, keep_other, sems):
    place = Place(where)
    x0, x1, payload = read(size, x_in)
    y0, y1, ranks, payload = section_step(
        size, place, place.section, 0, x0, x1, again_own[0], payload, mine, other, 0
    )
    keep(size, keep_mine, keep_other, x0, x1, ranks)
    copies = [
        pltpu.make_async_copy(keep_mine, hist_mine.at[pl.ds(0, 1)], sems.at[0]),
        pltpu.make_async_copy(keep_other, hist_other.at[pl.ds(0, 1)], sems.at[1]),
    ]
    for copy in copies:
        copy.start()
    write(size, out, y0, y1, payload)
    for copy in copies:
        copy.wait()


def second_kernel(size, where, x_in, again_peer, mine, other, out, hist_peer, keep_peer, sem):
    place = Place(where)
    x0, x1, payload = read(size, x_in)
    again = join_words(again_peer[:, : 2 * size.rank])
    y0, y1, ranks, sent = section_step(size, place, place.peer, 1, x0, x1, again, payload, mine, other, 2)
    keep_passed(size, keep_peer, x0, x1, ranks)
    copy = pltpu.make_async_copy(keep_peer, hist_peer.at[:, pl.ds(0, 1)], sem)
    copy.start()
    aligned = place.aligned
    sent = [jnp.where(aligned, sent[j], payload[j]) for j in range(size.slots)]
    write(size, out, jnp.where(aligned, y0, x0), jnp.where(aligned, y1, x1), sent)
    copy.wait()


def pair_kernel(size, step, where, x_in, feeds, again_own, again_peer, mine, other, *rest):
    final = step + 1 == size.steps
    if final:
        _, _, out, passed, hist_mine, hist_other, keep_mine, keep_other, sems = rest
    else:
        _, _, _, out, hist_mine, hist_other, hist_peer, keep_mine, keep_other, keep_peer, sems = rest
        passed = keep_peer
    half, kept, span = size.half, size.kept, 2 * size.rank
    place = Place(where)
    aligned = place.aligned
    x0, x1, payload = read(size, x_in)
    feed = feeds.at[where[4 + step]]
    x0 = jnp.where(place.at_end, feed[:, :half], x0)
    x1 = jnp.where(place.at_end, feed[:, half:], x1)
    tick = jnp.where(aligned, 2 * step, 2 * step - 1)
    now, before = (again_peer[:, i * span : (i + 1) * span] for i in (step, step - 1))
    again_peer = join_words(jnp.where(aligned, now, before))
    own = again_own[2 * step]
    at_peer = jnp.where(aligned, 0, 2)
    y0, y1, ranks, payload = section_step(
        size, place, jnp.where(aligned, place.section, place.peer), tick, x0, x1,
        jnp.where(aligned, own, again_peer), payload, mine, other, at_peer,
    )
    z0, z1, ranks_b, payload = section_step(
        size, place, jnp.where(aligned, place.peer, place.section), tick + 1, y0, y1,
        jnp.where(aligned, again_peer, own), payload, mine, other, 2 - at_peer,
    )
    keep(
        size, keep_mine, keep_other,
        jnp.where(aligned, x0, y0), jnp.where(aligned, x1, y1), jnp.where(aligned, ranks, ranks_b),
    )
    keep_passed(
        size, passed, jnp.where(aligned, y0, x0), jnp.where(aligned, y1, x1), jnp.where(aligned, ranks_b, ranks)
    )
    copies = [
        pltpu.make_async_copy(keep_mine, hist_mine.at[pl.ds(step, 1)], sems.at[0]),
        pltpu.make_async_copy(keep_other, hist_other.at[pl.ds(step, 1)], sems.at[1]),
    ]
    if not final:
        copies.append(pltpu.make_async_copy(keep_peer, hist_peer.at[:, pl.ds(step, 1)], sems.at[2]))
    for copy in copies:
        copy.start()
    if final:
        passed[0, 0, :, kept:] = z0
        passed[1, 0, :, kept:] = z1
    write(size, out, z0, z1, payload)
    for copy in copies:
        copy.wait()


def last_kernel(size, where, x_in, feeds, again_own, mine, other, last_mine, last_other):
    half, kept = size.half, size.kept
    place = Place(where)
    x0, x1, payload = read(size, x_in)
    feed = feeds.at[where[4 + size.steps]]
    x0 = jnp.where(place.at_end, feed[:, :half], x0)
    x1 = jnp.where(place.at_end, feed[:, half:], x1)
    tick = size.ticks - 1
    y0, y1, ranks, _ = section_step(
        size, place, place.section, tick, x0, x1, again_own[tick], payload, mine, other, 0
    )
    for ref, x, y in ((last_mine, x0, y0), (last_other, x1, y1)):
        ref[:, :half] = x
        ref[:, half:kept] = ranks
        ref[:, kept:] = y


def end_kernel(size, where, mine, sent, got, odd, odd_got, late, late_got, last_mine, last_other, last_got, stash, *outs):
    squeeze_grad, expand_grad, fwd, bwd = outs
    ticks, half, kept, rank, steps = size.ticks, size.half, size.kept, size.rank, size.steps
    place = Place(where)
    forward = place.forward

    def block(role, t, cols, part=0):
        here = place.role == role
        i = t // 2

        def pick(own, other):
            return jnp.where(here, own[:, cols], other[:, cols])

        if t % 2 == 0:
            return pick((mine, sent)[part].at[i], got.at[i])

        def passed(i):
            if i + 1 < steps:
                return pick(odd.at[part, i], odd_got.at[i])
            if i + 1 == steps:
                return pick(late.at[part, 0], late_got)
            return pick((last_mine, last_other)[part], last_got)

        return jnp.where(place.side == role, passed(i + 1), passed(i))

    lag = 2 * (place.sections - 1 - place.section) + 1
    ranks = jnp.concatenate([block(1, t, slice(half, kept), 1) for t in range(ticks)], axis=0)
    regated, hidden_grad = ranks[:, :rank], ranks[:, rank:]
    for lo in range(0, half, CHUNK):
        cols = slice(lo, min(lo + CHUNK, half))
        a = [block(0, t, cols) for t in range(ticks - 1)]
        u = []
        for t in range(ticks):
            at = stash[t, :, cols]
            for j in range((t + 1) // 2):
                at = jnp.where(lag == 2 * j + 1, a[t - 2 * j - 1], at)
            u.append(at)
        u = jnp.concatenate(u, axis=0)
        g = jnp.concatenate([block(1, t, cols) for t in range(ticks)], axis=0)
        squeeze_grad[:, cols] = (dot(hidden_grad, u, TN) * size.in_scale).astype(jnp.bfloat16)
        expand_grad[:, cols] = (dot(regated, g, TN) * size.out_scale).astype(jnp.bfloat16)

    def carry(role):
        here = place.role == role
        early = jnp.where(here, late[0, 0, :, kept:], late_got[:, kept:])
        final = jnp.where(here, last_mine[:, kept:], last_got[:, kept:])
        return jnp.where(place.side == role, final, early)

    fwd[...] = carry(0)
    bwd[...] = carry(1)


def params():
    return pltpu.CompilerParams(vmem_limit_bytes=24 * 1024 * 1024)


def shape(*dims, dtype=jnp.bfloat16):
    return jax.ShapeDtypeStruct(dims, dtype)


def shards(
    activations,
    cotangent,
    squeeze_old,
    expand_old,
    squeeze_late,
    expand_late,
    stash_inputs,
    forward_in,
    backward_in,
):
    sections = lax.axis_size("pipe")
    replicas = lax.axis_size("dp")
    section = lax.axis_index("pipe")
    role = lax.axis_index("mp")
    half, rank = squeeze_old.shape[1], squeeze_old.shape[2]
    ticks, rows = stash_inputs.shape[2], stash_inputs.shape[3]
    size = Sizes(ticks, rows, rank, half)
    bf16, f32 = jnp.bfloat16, jnp.float32
    everyone = range(sections)

    def send(x, pairs):
        return lax.ppermute(x, ("pipe", "mp"), [(a * 2 + b, c * 2 + d) for (a, b), (c, d) in pairs])

    def swap(x):
        return lax.ppermute(x, "mp", [(0, 1), (1, 0)])

    def to_peer(x, senders):
        return send(x, [((s, c), (s ^ 1, c)) for s, c in senders])

    def tied(x, *others):
        return lax.optimization_barrier((x, *others))[0]

    def call(body, name, outs, in_specs, out_specs, scratch=(), aliases=None):
        return pl.pallas_call(
            functools.partial(body, size),
            out_shape=outs,
            in_specs=in_specs,
            out_specs=out_specs,
            scratch_shapes=list(scratch),
            input_output_aliases=aliases or {},
            compiler_params=params(),
            cost_estimate=pl.CostEstimate(
                flops=8 * rows * size.width * rank, bytes_accessed=8 * size.width * rank, transcendentals=0
            ),
            name=name,
        )

    side = section % 2
    where = jnp.stack([section, role, jnp.int32(sections), side]).astype(jnp.int32)
    forward = role == 0
    squeeze, expand = squeeze_old[0].T, expand_old[0]
    stash = stash_inputs[0, 0]
    fwd_in, bwd_in = forward_in[0, 0], backward_in[0, 0]
    acts, cots = activations[0], cotangent[0]
    both = [(s, c) for s in everyone for c in (0, 1)]

    squeeze_peer = to_peer(squeeze, both)
    own = lax.optimization_barrier(jnp.stack([squeeze, expand]))
    other = swap(own)
    squeeze_peer_other = swap(squeeze_peer)
    partial = call(
        stash_kernel, "stashed", shape(ticks, rows, rank, dtype=f32), [VMEM, VMEM], VMEM
    )(stash, squeeze)
    again_own = partial + swap(partial)
    words = jnp.concatenate([split_words(again_own[t]) for t in range(1, ticks, 2)], axis=1)
    words = jnp.pad(words, ((0, 0), (0, half - words.shape[1])))
    expand_peer = to_peer(tied(jnp.concatenate([expand, words], axis=0), squeeze_peer), both)
    again_peer = expand_peer[rank:, : size.steps * 2 * rank]

    entering_full = jnp.concatenate(
        [jnp.where(forward, acts, cots), swap(jnp.where(forward, cots, acts))], axis=1
    )
    per_tick = rows // acts.shape[0]

    ends = {}
    for b in range(ticks):
        to = b % 2 if b + 1 < ticks else 0
        ends.setdefault((to, 0), []).append(b)
        ends.setdefault((sections - 1 - to, 1), []).append(b)
    turn = {}
    trips = [[] for _ in range(ticks)]
    for (to, core), blocks in ends.items():
        local = [b for b in blocks if all(b * per_tick + m == to for m in range(per_tick))]
        for n, b in enumerate(b for b in blocks if b not in local):
            trip, swapped = n // 2, n % 2
            turn[to, core, b] = 1 + 2 * trip + swapped
            trips[trip].append((b, core, (to, core ^ swapped)))
        for b in local:
            turn[to, core, b] = 0

    def fed(trip):
        pieces = []
        for m in range(per_tick):
            moves = [((b * per_tick + m, core), to) for b, core, to in trip]
            came = send(entering_full, [(a, b) for a, b in moves if a != b])
            for a, b in moves:
                if a == b:
                    came = jnp.where(jnp.logical_and(section == a[0], role == a[1]), entering_full, came)
            pieces.append(came)
        return jnp.concatenate(pieces, axis=0)

    feeds = [jnp.tile(entering_full, (per_tick, 1))]
    for trip in trips:
        if trip:
            feeds.append(fed(trip))
            feeds.append(swap(feeds[-1]))
    feeds = jnp.stack(feeds)

    def reads(b_of):
        index = jnp.int32(0)
        for (to, core), blocks in ends.items():
            b = b_of(to, core)
            if b in blocks:
                here = jnp.logical_and(section == to, role == core)
                index = jnp.where(here, jnp.int32(turn[to, core, b]), index)
        return index

    def block_at(step):
        def b_of(to, core):
            side_to = to if core == 0 else sections - 1 - to
            return ticks - 1 if step == size.steps else 2 * step - side_to

        return b_of

    where = jnp.concatenate([where, jnp.stack([reads(block_at(step)) for step in range(size.steps + 1)])])
    first_end = section == jnp.where(forward, 0, sections - 1)
    first_feed = lax.dynamic_index_in_dim(feeds, where[4], 0, keepdims=False)
    x = jnp.concatenate([jnp.where(forward, fwd_in, bwd_in), swap(jnp.where(forward, bwd_in, fwd_in))], axis=1)
    x = jnp.concatenate([jnp.where(first_end, first_feed, x), jnp.zeros((rows, size.message - size.width), bf16)], axis=1)

    hist_shapes = (shape(size.steps, rows, half), shape(size.steps, rows, size.kept))
    hist_peer_shape = shape(2, size.steps - 1, rows, size.kept)
    keep_own = (pltpu.VMEM((1, rows, half), bf16), pltpu.VMEM((1, rows, size.kept), bf16))
    keep_peer = (pltpu.VMEM((2, 1, rows, size.kept), bf16),)

    def sems(n):
        return (pltpu.SemaphoreType.DMA((n,)),)

    late_own = jnp.stack([squeeze_late[0, 0].T, expand_late[0, 0]])
    if replicas == 2:
        total = late_own.astype(f32) + lax.ppermute(late_own, "dp", [(0, 1), (1, 0)]).astype(f32)
    else:
        total = lax.psum(late_own, "dp").astype(f32)
    squeeze_new = (squeeze.astype(f32) - STEP_RATE * total[0] / replicas).astype(bf16)
    expand_new = (expand.astype(f32) - STEP_RATE * total[1] / replicas).astype(bf16)

    ring = (
        [((s, 0), (s + 2, 0)) for s in range(sections - 2)]
        + [((sections - 2, 0), (sections - 1, 1)), ((sections - 1, 0), (sections - 2, 1))]
        + [((s, 1), (s - 2, 1)) for s in range(2, sections)]
    )
    ring_last = (
        [((s, 0), (s + 1, 0)) for s in range(1, sections - 1, 2)]
        + [((sections - 1, 0), (sections - 1, 1))]
        + [((s, 1), (s - 1, 1)) for s in range(2, sections, 2)]
    )

    x, hist_mine, hist_other = call(
        first_kernel, "first", (shape(rows, size.message), *hist_shapes),
        [SMEM, VMEM, VMEM, VMEM, VMEM], (VMEM, ANY, ANY), keep_own + sems(2),
    )(where, x, again_own, own, other)
    expand_peer_other = swap(tied(expand_peer, x))[:rank]
    mine_all = jnp.concatenate([own, squeeze_peer[None], expand_peer[None, :rank]], axis=0)
    other_all = jnp.concatenate([other, squeeze_peer_other[None], expand_peer_other[None]], axis=0)
    x, hist_peer = call(
        second_kernel, "second", (shape(rows, size.message), hist_peer_shape),
        [SMEM, VMEM, VMEM, VMEM, VMEM], (VMEM, ANY), (*keep_peer, pltpu.SemaphoreType.DMA),
    )(where, tied(x, feeds), again_peer, mine_all, other_all)
    x = send(x, ring)
    for step in range(1, size.steps):
        final = step + 1 == size.steps
        if step == 1:
            x = tied(x, squeeze_new)
        if step == 2:
            x = tied(x, expand_new)
        body = functools.partial(lambda step, size, *refs: pair_kernel(size, step, *refs), step)
        ins = (where, x, feeds, again_own, again_peer, mine_all, other_all, hist_mine, hist_other)
        if final:
            x, passed, hist_mine, hist_other = call(
                body, f"pair{step}",
                (shape(rows, size.message), shape(2, 1, rows, size.kept + half), *hist_shapes),
                [SMEM] + [VMEM] * 6 + [ANY] * 2, (VMEM, VMEM, ANY, ANY), keep_own + sems(2), {7: 2, 8: 3},
            )(*ins)
        else:
            x, hist_mine, hist_other, hist_peer = call(
                body, f"pair{step}",
                (shape(rows, size.message), *hist_shapes, hist_peer_shape),
                [SMEM] + [VMEM] * 6 + [ANY] * 3, (VMEM, ANY, ANY, ANY), keep_own + keep_peer + sems(3),
                {7: 1, 8: 2, 9: 3},
            )(*ins, hist_peer)
        x = send(x, ring_last if final else ring)
    odd = to_peer(hist_peer, both)
    late = to_peer(passed, both)
    odd_got, late_got = swap(odd[1]), swap(late[1, 0])
    hist_got = swap(hist_other)
    last_mine, last_other = call(
        last_kernel, "last", (shape(rows, size.kept + half), shape(rows, size.kept + half)),
        [SMEM, VMEM, VMEM, VMEM, VMEM, VMEM], (VMEM, VMEM),
    )(where, x, feeds, again_own, own, other)
    last_got = swap(last_other)
    squeeze_grad, expand_grad, fwd_carry, bwd_carry = call(
        end_kernel, "finish",
        (shape(rank, half), shape(rank, half), shape(rows, half), shape(rows, half)),
        [SMEM] + [VMEM] * 11, (VMEM,) * 4,
    )(where, hist_mine, hist_other, hist_got, odd, odd_got, late, late_got, last_mine, last_other, last_got, stash)
    return (
        squeeze_new.T[None],
        expand_new[None],
        squeeze_grad.T[None, None],
        expand_grad[None, None],
        fwd_carry[None, None],
        bwd_carry[None, None],
    )


def solution(mesh):
    placed = (
        P("dp", "pipe", "mp"),
        P("dp", "pipe", "mp"),
        P("pipe", "mp", None),
        P("pipe", None, "mp"),
        P("dp", "pipe", "mp", None),
        P("dp", "pipe", None, "mp"),
        P("dp", "pipe", None, None, "mp"),
        P("dp", "pipe", None, "mp"),
        P("dp", "pipe", None, "mp"),
    )
    return jax.shard_map(
        shards,
        mesh=mesh,
        in_specs=placed,
        out_specs=(
            P("pipe", "mp", None),
            P("pipe", None, "mp"),
            P("dp", "pipe", "mp", None),
            P("dp", "pipe", None, "mp"),
            P("dp", "pipe", None, "mp"),
            P("dp", "pipe", None, "mp"),
        ),
        check_vma=False,
    )
```

```python
import functools
import math

import jax
import jax.numpy as jnp
from jax import lax
from jax.experimental import pallas as pl
from jax.experimental.pallas import tpu as pltpu
from jax.sharding import PartitionSpec as P

BRANCH_SCALE = 0.25
STEP_RATE = 0.5
CHUNK = 512

VMEM = pl.BlockSpec(memory_space=pltpu.VMEM)
SMEM = pl.BlockSpec(memory_space=pltpu.SMEM)
ANY = pl.BlockSpec(memory_space=pl.ANY)
NT = (((1,), (1,)), ((), ()))
TN = (((0,), (0,)), ((), ()))


def dot(a, b, dims=(((1,), (0,)), ((), ()))):
    return lax.dot_general(a, b, dims, preferred_element_type=jnp.float32)


def gelu_and_slope(x):
    c = math.sqrt(2.0 / math.pi)
    t = jnp.tanh(c * (x + 0.044715 * (x * x * x)))
    half = 0.5 * (1.0 + t)
    slope = half + 0.5 * x * (1.0 - t * t) * (c * (1.0 + 3 * 0.044715 * (x * x)))
    return x * half, slope


def split_words(x):
    hi = x.astype(jnp.bfloat16)
    lo = (x - hi.astype(jnp.float32)).astype(jnp.bfloat16)
    return jnp.concatenate([hi, lo], axis=1)


def join_words(words):
    rank = words.shape[1] // 2
    return words[:, :rank].astype(jnp.float32) + words[:, rank:].astype(jnp.float32)


class Place:
    def __init__(self, where):
        self.section, self.role, self.sections = where[0], where[1], where[2]
        self.side = where[3]
        self.forward = self.role == 0
        self.aligned = self.side == self.role
        self.peer = self.section + 1 - 2 * self.side
        pair = jnp.where(self.forward, self.section, self.sections - 1 - self.section)
        self.at_end = pair < 2


class Sizes:
    def __init__(self, ticks, rows, rank, half):
        self.ticks, self.rows, self.rank, self.half = ticks, rows, rank, half
        self.steps = ticks // 2
        self.slots = ticks // 2
        self.width = 2 * half
        self.message = 2 * half + self.slots * 2 * rank
        self.kept = half + 2 * rank
        self.in_scale = 1.0 / math.sqrt(2 * half)
        self.out_scale = BRANCH_SCALE / math.sqrt(rank)


def section_step(size, place, section, tick, x0, x1, again, payload, mine, other, at):
    forward = place.forward
    back = place.sections - 1 - section
    first, second = at + place.role, at + 1 - place.role
    h = (dot(x0, mine[first], NT) + dot(x1, other[first], NT)) * jnp.where(
        forward, size.in_scale, size.out_scale
    )
    for j in range(size.slots):
        ready = jnp.logical_and(back == j, tick >= 2 * j + 1)
        again = jnp.where(ready, join_words(payload[j]), again)
    value, slope = gelu_and_slope(jnp.where(forward, h, again))
    z = jnp.where(forward, value, h * slope).astype(jnp.bfloat16)
    ranks = jnp.concatenate([value.astype(jnp.bfloat16), z], axis=1)
    scale = jnp.where(forward, size.out_scale, size.in_scale)
    y0 = (x0.astype(jnp.float32) + dot(z, mine[second]) * scale).astype(jnp.bfloat16)
    y1 = (x1.astype(jnp.float32) + dot(z, other[second]) * scale).astype(jnp.bfloat16)
    words = split_words(h)
    payload = [jnp.where(jnp.logical_and(forward, back == j), words, payload[j]) for j in range(size.slots)]
    return y0, y1, ranks, payload


def read(size, ref):
    half, span = size.half, 2 * size.rank
    payload = [ref[:, 2 * half + j * span : 2 * half + (j + 1) * span] for j in range(size.slots)]
    return ref[:, :half], ref[:, half : 2 * half], payload


def write(size, ref, y0, y1, payload):
    half, span = size.half, 2 * size.rank
    ref[:, :half] = y0
    ref[:, half : 2 * half] = y1
    for j in range(size.slots):
        ref[:, 2 * half + j * span : 2 * half + (j + 1) * span] = payload[j]


def stash_kernel(size, stash, squeeze, partial):
    ticks, rows, half = stash.shape
    whole = dot(stash[...].reshape(ticks * rows, half), squeeze[...], NT) * size.in_scale
    for t in range(ticks):
        partial[t] = whole[t * rows : (t + 1) * rows]


def keep(size, keep_mine, keep_other, x0, x1, ranks):
    keep_mine[0] = x0
    keep_other[0, :, : size.half] = x1
    keep_other[0, :, size.half :] = ranks


def keep_passed(size, ref, x0, x1, ranks):
    half, kept = size.half, size.kept
    for part, x in enumerate((x0, x1)):
        ref[part, :, :half] = x
        ref[part, :, half:kept] = ranks


def entering(place, size, step, x0, x1, where, feeds, at_end):
    index = where[4 + step]
    for n, ref in feeds.items():
        here = jnp.logical_and(at_end, index == n)
        x0 = jnp.where(here, ref[:, : size.half], x0)
        x1 = jnp.where(here, ref[:, size.half :], x1)
    return x0, x1


def first_kernel(size, where, x_in, again_own, mine, other, out, hist_mine, hist_other, keep_mine, keep_other, sems):
    place = Place(where)
    x0, x1, payload = read(size, x_in)
    y0, y1, ranks, payload = section_step(
        size, place, place.section, 0, x0, x1, again_own[0], payload, mine, other, 0
    )
    keep(size, keep_mine, keep_other, x0, x1, ranks)
    copies = [
        pltpu.make_async_copy(keep_mine, hist_mine.at[pl.ds(0, 1)], sems.at[0]),
        pltpu.make_async_copy(keep_other, hist_other.at[pl.ds(0, 1)], sems.at[1]),
    ]
    for copy in copies:
        copy.start()
    write(size, out, y0, y1, payload)
    for copy in copies:
        copy.wait()


def second_kernel(size, where, x_in, again_peer, mine, other, out, held):
    place = Place(where)
    x0, x1, payload = read(size, x_in)
    y0, y1, ranks, sent = section_step(
        size, place, place.peer, 1, x0, x1, again_peer[0], payload, mine, other, 2
    )
    keep_passed(size, held, x0, x1, ranks)
    aligned = place.aligned
    sent = [jnp.where(aligned, sent[j], payload[j]) for j in range(size.slots)]
    write(size, out, jnp.where(aligned, y0, x0), jnp.where(aligned, y1, x1), sent)


def pair_kernel(size, step, turns, where, x_in, held, passed, again_own, again_peer, mine, other, *rest):
    feeds = dict(zip(turns, rest))
    _, _, out, held_out, passed_out, hist_mine, hist_other, keep_mine, keep_other, sems = rest[len(turns) :]
    half, kept = size.half, size.kept
    place = Place(where)
    aligned = place.aligned
    x0, x1, payload = read(size, x_in)
    x0, x1 = entering(place, size, step, x0, x1, where, feeds, place.at_end)
    tick = jnp.where(aligned, 2 * step, 2 * step - 1)
    again_peer = again_peer[jnp.where(aligned, step, step - 1)]
    own = again_own[2 * step]
    at_peer = jnp.where(aligned, 0, 2)
    y0, y1, ranks, payload = section_step(
        size, place, jnp.where(aligned, place.section, place.peer), tick, x0, x1,
        jnp.where(aligned, own, again_peer), payload, mine, other, at_peer,
    )
    z0, z1, ranks_b, sent = section_step(
        size, place, jnp.where(aligned, place.peer, place.section), tick + 1, y0, y1,
        jnp.where(aligned, again_peer, own), payload, mine, other, 2 - at_peer,
    )
    keep(
        size, keep_mine, keep_other,
        jnp.where(aligned, x0, y0), jnp.where(aligned, x1, y1), jnp.where(aligned, ranks, ranks_b),
    )
    copies = [
        pltpu.make_async_copy(keep_mine, hist_mine.at[pl.ds(step, 1)], sems.at[0]),
        pltpu.make_async_copy(keep_other, hist_other.at[pl.ds(step, 1)], sems.at[1]),
    ]
    for copy in copies:
        copy.start()
    final = step + 1 == size.steps
    for part, (first, second) in enumerate(((x0, y0), (x1, y1))):
        if not final:
            held_out[part, :, :half] = second
            held_out[part, :, half:] = ranks_b
        if step == 2:
            passed_out[0, part] = passed[0, part]
        at = passed_out.at[step - 1 if not final else 0, part]
        at[:, :half] = jnp.where(aligned, held[part, :, :half], first)
        at[:, half:] = jnp.where(aligned, held[part, :, half:], ranks)
    if final:
        held_out[...] = jnp.zeros(held_out.shape, held_out.dtype)
        sent = [jnp.where(aligned, payload[j], sent[j]) for j in range(size.slots)]
        z0, z1 = jnp.where(aligned, y0, z0), jnp.where(aligned, y1, z1)
    write(size, out, z0, z1, sent)
    for copy in copies:
        copy.wait()


def last_kernel(size, turns, where, x_in, again_own, mine, other, *rest):
    feeds = dict(zip(turns, rest))
    last_mine, last_other = rest[len(turns) :]
    half, kept = size.half, size.kept
    place = Place(where)
    x0, x1, payload = read(size, x_in)
    at_end = jnp.where(place.forward, place.section, place.sections - 1 - place.section) == 0
    x0, x1 = entering(place, size, size.steps, x0, x1, where, feeds, at_end)
    tick = size.ticks - 1
    y0, y1, ranks, _ = section_step(
        size, place, place.section, tick, x0, x1, again_own[tick], payload, mine, other, 0
    )
    for ref, x, y in ((last_mine, x0, y0), (last_other, x1, y1)):
        ref[:, :half] = x
        ref[:, half:kept] = ranks
        ref[:, kept:] = y


def end_kernel(size, where, mine, sent, got, odd, odd_got, late, late_got, last_mine, last_other, last_got, stash, *outs):
    squeeze_grad, expand_grad, fwd, bwd = outs
    ticks, half, kept, rank = size.ticks, size.half, size.kept, size.rank
    place = Place(where)

    def block(role, t, cols, part=0):
        here = place.role == role
        i = t // 2

        def pick(own, other):
            return jnp.where(here, own[:, cols], other[:, cols])

        if t % 2 == 0:
            return pick((mine, sent)[part].at[i], got.at[i])
        if t + 1 == ticks:
            return pick((last_mine, last_other)[part], last_got)
        if t + 3 == ticks:
            return pick(late.at[part], late_got)
        return pick(odd.at[i, part], odd_got.at[i])

    lag = 2 * (place.sections - 1 - place.section) + 1
    ranks = jnp.concatenate([block(1, t, slice(half, kept), 1) for t in range(ticks)], axis=0)
    regated, hidden_grad = ranks[:, :rank], ranks[:, rank:]
    for lo in range(0, half, CHUNK):
        cols = slice(lo, min(lo + CHUNK, half))
        a = [block(0, t, cols) for t in range(ticks - 1)]
        u = []
        for t in range(ticks):
            at = stash[t, :, cols]
            for j in range((t + 1) // 2):
                at = jnp.where(lag == 2 * j + 1, a[t - 2 * j - 1], at)
            u.append(at)
        u = jnp.concatenate(u, axis=0)
        g = jnp.concatenate([block(1, t, cols) for t in range(ticks)], axis=0)
        squeeze_grad[:, cols] = (dot(hidden_grad, u, TN) * size.in_scale).astype(jnp.bfloat16)
        expand_grad[:, cols] = (dot(regated, g, TN) * size.out_scale).astype(jnp.bfloat16)

    def carry(role):
        return jnp.where(place.role == role, last_mine[:, kept:], last_got[:, kept:])

    fwd[...] = carry(0)
    bwd[...] = carry(1)


def params():
    return pltpu.CompilerParams(vmem_limit_bytes=24 * 1024 * 1024)


def shape(*dims, dtype=jnp.bfloat16):
    return jax.ShapeDtypeStruct(dims, dtype)


def shards(
    activations,
    cotangent,
    squeeze_old,
    expand_old,
    squeeze_late,
    expand_late,
    stash_inputs,
    forward_in,
    backward_in,
):
    sections = lax.axis_size("pipe")
    replicas = lax.axis_size("dp")
    section = lax.axis_index("pipe")
    role = lax.axis_index("mp")
    half, rank = squeeze_old.shape[1], squeeze_old.shape[2]
    ticks, rows = stash_inputs.shape[2], stash_inputs.shape[3]
    size = Sizes(ticks, rows, rank, half)
    bf16, f32 = jnp.bfloat16, jnp.float32
    everyone = range(sections)

    def send(x, pairs):
        return lax.ppermute(x, ("pipe", "mp"), [(a * 2 + b, c * 2 + d) for (a, b), (c, d) in pairs])

    def swap(x):
        return lax.ppermute(x, "mp", [(0, 1), (1, 0)])

    def to_peer(x, senders):
        return send(x, [((s, c), (s ^ 1, c)) for s, c in senders])

    def tied(x, *others):
        return lax.optimization_barrier((x, *others))[0]

    def call(body, name, outs, in_specs, out_specs, scratch=(), aliases=None):
        return pl.pallas_call(
            functools.partial(body, size),
            out_shape=outs,
            in_specs=in_specs,
            out_specs=out_specs,
            scratch_shapes=list(scratch),
            input_output_aliases=aliases or {},
            compiler_params=params(),
            cost_estimate=pl.CostEstimate(
                flops=8 * rows * size.width * rank, bytes_accessed=8 * size.width * rank, transcendentals=0
            ),
            name=name,
        )

    side = section % 2
    where = jnp.stack([section, role, jnp.int32(sections), side]).astype(jnp.int32)
    forward = role == 0
    squeeze, expand = squeeze_old[0].T, expand_old[0]
    stash = stash_inputs[0, 0]
    fwd_in, bwd_in = forward_in[0, 0], backward_in[0, 0]
    acts, cots = activations[0], cotangent[0]
    both = [(s, c) for s in everyone for c in (0, 1)]

    own = lax.optimization_barrier(jnp.stack([squeeze, expand]))
    peer = to_peer(own, both)
    other = swap(own)

    partial = call(
        stash_kernel, "stashed", shape(ticks, rows, rank, dtype=f32), [VMEM, VMEM], VMEM
    )(stash, squeeze)
    again_own = partial + swap(partial)
    again_peer = to_peer(again_own[1::2], [(s, 1) for s in everyone])

    entering_full = jnp.concatenate(
        [jnp.where(forward, acts, cots), swap(jnp.where(forward, cots, acts))], axis=1
    )
    per_tick = rows // acts.shape[0]

    ends = {}
    for b in range(ticks):
        to = b % 2 if b + 1 < ticks else 0
        ends.setdefault((to, 0), []).append(b)
        ends.setdefault((sections - 1 - to, 1), []).append(b)
    turn = {}
    trips = [[] for _ in range(ticks)]
    for (to, core), blocks in ends.items():
        local = [b for b in blocks if all(b * per_tick + m == to for m in range(per_tick))]
        for n, b in enumerate(b for b in blocks if b not in local):
            trip, swapped = n // 2, n % 2
            turn[to, core, b] = 1 + 2 * trip + swapped
            trips[trip].append((b, core, (to, core ^ swapped)))
        for b in local:
            turn[to, core, b] = 0

    def fed(trip):
        pieces = []
        for m in range(per_tick):
            moves = [((b * per_tick + m, core), to) for b, core, to in trip]
            came = send(entering_full, [(a, b) for a, b in moves if a != b])
            for a, b in moves:
                if a == b:
                    came = jnp.where(jnp.logical_and(section == a[0], role == a[1]), entering_full, came)
            pieces.append(came)
        return jnp.concatenate(pieces, axis=0)

    feeds = [jnp.tile(entering_full, (per_tick, 1))]
    for trip in trips:
        if trip:
            feeds.append(fed(trip))
            feeds.append(swap(feeds[-1]))

    def reads(b_of):
        index = jnp.int32(0)
        for (to, core), blocks in ends.items():
            b = b_of(to, core)
            if b in blocks:
                here = jnp.logical_and(section == to, role == core)
                index = jnp.where(here, jnp.int32(turn[to, core, b]), index)
        return index

    def used(b_of):
        turns = {turn[to, core, b_of(to, core)] for (to, core), blocks in ends.items() if b_of(to, core) in blocks}
        return tuple(sorted(turns))

    def block_at(step):
        def b_of(to, core):
            side_to = to if core == 0 else sections - 1 - to
            return ticks - 1 if step == size.steps else 2 * step - side_to

        return b_of

    where = jnp.concatenate([where, jnp.stack([reads(block_at(step)) for step in range(size.steps + 1)])])
    first_end = section == jnp.where(forward, 0, sections - 1)
    first_feed = feeds[0]
    for n in used(block_at(0)):
        first_feed = jnp.where(where[4] == n, feeds[n], first_feed)
    x = jnp.concatenate([jnp.where(forward, fwd_in, bwd_in), swap(jnp.where(forward, bwd_in, fwd_in))], axis=1)
    x = jnp.concatenate([jnp.where(first_end, first_feed, x), jnp.zeros((rows, size.message - size.width), bf16)], axis=1)

    hist_shapes = (shape(size.steps, rows, half), shape(size.steps, rows, size.kept))
    odd_shape = (2, rows, size.kept)
    keep_own = (
        pltpu.VMEM((1, rows, half), bf16),
        pltpu.VMEM((1, rows, size.kept), bf16),
        pltpu.SemaphoreType.DMA((2,)),
    )

    def averaged(old, late):
        if replicas == 2:
            came = lax.ppermute(late, "dp", [(0, 1), (1, 0)])
            total = late.astype(f32) + came.astype(f32)
        else:
            came = lax.psum(late, "dp")
            total = came.astype(f32)
        return (old.astype(f32) - STEP_RATE * total / replicas).astype(bf16), came

    squeeze_new, came = averaged(squeeze, squeeze_late[0, 0].T)
    expand_new, _ = averaged(expand, tied(expand_late[0, 0], came))

    ring = (
        [((s, 0), (s + 2, 0)) for s in range(sections - 2)]
        + [((sections - 2, 0), (sections - 1, 1)), ((sections - 1, 0), (sections - 2, 1))]
        + [((s, 1), (s - 2, 1)) for s in range(2, sections)]
    )
    ring_last = (
        [((s, 0), (s + 1, 0)) for s in range(sections - 1)]
        + [((sections - 1, 0), (sections - 1, 1))]
        + [((s, 1), (s - 1, 1)) for s in range(1, sections)]
    )
    passing = [(s, c) for s, c in both if c == 1 or (s ^ 1) >= sections - size.slots]
    x, hist_mine, hist_other = call(
        first_kernel, "first", (shape(rows, size.message), *hist_shapes),
        [SMEM, VMEM, VMEM, VMEM, VMEM], (VMEM, ANY, ANY), keep_own,
    )(where, x, again_own, own, other)
    peer_other = swap(peer)
    mine_all = jnp.concatenate([own, tied(peer, x)], axis=0)
    other_all = jnp.concatenate([other, peer_other], axis=0)
    x, held = call(
        second_kernel, "second", (shape(rows, size.message), shape(*odd_shape)),
        [SMEM, VMEM, VMEM, VMEM, VMEM], (VMEM, VMEM),
    )(where, tied(x, *feeds[1::2]), again_peer, mine_all, other_all)
    x = send(x, ring)
    passed = jnp.zeros((1, *odd_shape), bf16)
    for step in range(1, size.steps):
        final = step + 1 == size.steps
        if step == 2:
            x = tied(x, squeeze_new)
        if step == 3:
            x = tied(x, expand_new)
        turns = used(block_at(step))
        body = functools.partial(lambda step, turns, size, *refs: pair_kernel(size, step, turns, *refs), step, turns)
        x, held, passed_now, hist_mine, hist_other = call(
            body, f"pair{step}",
            (
                shape(rows, size.message),
                shape(*((8, 128) if final else odd_shape)),
                shape(1 if final else step, *odd_shape),
                *hist_shapes,
            ),
            [SMEM] + [VMEM] * (7 + len(turns)) + [ANY] * 2, (VMEM, VMEM, VMEM, ANY, ANY), keep_own,
            {8 + len(turns): 3, 9 + len(turns): 4},
        )(
            where, x, held, passed, again_own, again_peer, mine_all, other_all, *(feeds[n] for n in turns),
            hist_mine, hist_other,
        )
        x = send(x, ring_last if final else ring)
        if final:
            odd, late = to_peer(passed, passing), to_peer(passed_now[0], passing)
        passed = passed_now
    odd_got, late_got = swap(odd[:, 1]), swap(late[1])
    hist_got = swap(hist_other)
    turns = used(block_at(size.steps))
    last_mine, last_other = call(
        functools.partial(lambda turns, size, *refs: last_kernel(size, turns, *refs), turns), "last",
        (shape(rows, size.kept + half), shape(rows, size.kept + half)),
        [SMEM] + [VMEM] * (4 + len(turns)), (VMEM, VMEM),
    )(where, tied(x, odd), again_own, own, other, *(feeds[n] for n in turns))
    last_got = swap(last_other)
    squeeze_grad, expand_grad, fwd_carry, bwd_carry = call(
        end_kernel, "finish",
        (shape(rank, half), shape(rank, half), shape(rows, half), shape(rows, half)),
        [SMEM] + [VMEM] * 11, (VMEM,) * 4,
    )(where, hist_mine, hist_other, hist_got, odd, odd_got, late, late_got, last_mine, last_other, last_got, stash)
    return (
        squeeze_new.T[None],
        expand_new[None],
        squeeze_grad.T[None, None],
        expand_grad[None, None],
        fwd_carry[None, None],
        bwd_carry[None, None],
    )


def solution(mesh):
    placed = (
        P("dp", "pipe", "mp"),
        P("dp", "pipe", "mp"),
        P("pipe", "mp", None),
        P("pipe", None, "mp"),
        P("dp", "pipe", "mp", None),
        P("dp", "pipe", None, "mp"),
        P("dp", "pipe", None, None, "mp"),
        P("dp", "pipe", None, "mp"),
        P("dp", "pipe", None, "mp"),
    )
    return jax.shard_map(
        shards,
        mesh=mesh,
        in_specs=placed,
        out_specs=(
            P("pipe", "mp", None),
            P("pipe", None, "mp"),
            P("dp", "pipe", "mp", None),
            P("dp", "pipe", None, "mp"),
            P("dp", "pipe", None, "mp"),
            P("dp", "pipe", None, "mp"),
        ),
        check_vma=False,
    )
```

```python
import functools
import math

import jax
import jax.numpy as jnp
from jax import lax
from jax.experimental import pallas as pl
from jax.experimental.pallas import tpu as pltpu
from jax.sharding import PartitionSpec as P

BRANCH_SCALE = 0.25
STEP_RATE = 0.5
CHUNK = 512

VMEM = pl.BlockSpec(memory_space=pltpu.VMEM)
SMEM = pl.BlockSpec(memory_space=pltpu.SMEM)
ANY = pl.BlockSpec(memory_space=pl.ANY)
NT = (((1,), (1,)), ((), ()))
TN = (((0,), (0,)), ((), ()))


def dot(a, b, dims=(((1,), (0,)), ((), ()))):
    return lax.dot_general(a, b, dims, preferred_element_type=jnp.float32)


def gelu_and_slope(x):
    c = math.sqrt(2.0 / math.pi)
    t = jnp.tanh(c * (x + 0.044715 * (x * x * x)))
    half = 0.5 * (1.0 + t)
    slope = half + 0.5 * x * (1.0 - t * t) * (c * (1.0 + 3 * 0.044715 * (x * x)))
    return x * half, slope


def split_words(x):
    hi = x.astype(jnp.bfloat16)
    lo = (x - hi.astype(jnp.float32)).astype(jnp.bfloat16)
    return jnp.concatenate([hi, lo], axis=1)


def join_words(words):
    rank = words.shape[1] // 2
    return words[:, :rank].astype(jnp.float32) + words[:, rank:].astype(jnp.float32)


class Place:
    def __init__(self, where):
        self.section, self.role, self.sections = where[0], where[1], where[2]
        self.side = where[3]
        self.forward = self.role == 0
        self.aligned = self.side == self.role
        self.peer = self.section + 1 - 2 * self.side
        pair = jnp.where(self.forward, self.section, self.sections - 1 - self.section)
        self.at_end = pair < 2


class Sizes:
    def __init__(self, ticks, rows, rank, half):
        self.ticks, self.rows, self.rank, self.half = ticks, rows, rank, half
        self.steps = ticks // 2
        self.slots = ticks // 2
        self.width = 2 * half
        self.message = 2 * half + self.slots * 2 * rank
        self.kept = half + 2 * rank
        self.in_scale = 1.0 / math.sqrt(2 * half)
        self.out_scale = BRANCH_SCALE / math.sqrt(rank)


def stacked(place, mine, other, at=0):
    into, out = at + place.role, at + 1 - place.role
    return (lambda: mine[into]), (lambda: other[into]), (lambda: mine[out]), (lambda: other[out])


def separate(place, squeeze0, squeeze1, expand0, expand1):
    def either(a, b):
        return lambda: jnp.where(place.forward, a[...], b[...])

    return either(squeeze0, expand0), either(squeeze1, expand1), either(expand0, squeeze0), either(expand1, squeeze1)


def section_step(size, place, section, tick, x0, x1, again, payload, weights):
    forward = place.forward
    back = place.sections - 1 - section
    into0, into1, from0, from1 = weights
    h = (dot(x0, into0(), NT) + dot(x1, into1(), NT)) * jnp.where(
        forward, size.in_scale, size.out_scale
    )
    for j in range(size.slots):
        ready = jnp.logical_and(back == j, tick >= 2 * j + 1)
        again = jnp.where(ready, join_words(payload[j]), again)
    value, slope = gelu_and_slope(jnp.where(forward, h, again))
    z = jnp.where(forward, value, h * slope).astype(jnp.bfloat16)
    ranks = jnp.concatenate([value.astype(jnp.bfloat16), z], axis=1)
    scale = jnp.where(forward, size.out_scale, size.in_scale)
    y0 = (x0.astype(jnp.float32) + dot(z, from0()) * scale).astype(jnp.bfloat16)
    y1 = (x1.astype(jnp.float32) + dot(z, from1()) * scale).astype(jnp.bfloat16)
    words = split_words(h)
    payload = [jnp.where(jnp.logical_and(forward, back == j), words, payload[j]) for j in range(size.slots)]
    return y0, y1, ranks, payload


def read(size, ref):
    half, span = size.half, 2 * size.rank
    payload = [ref[:, 2 * half + j * span : 2 * half + (j + 1) * span] for j in range(size.slots)]
    return ref[:, :half], ref[:, half : 2 * half], payload


def write(size, ref, y0, y1, payload):
    half, span = size.half, 2 * size.rank
    ref[:, :half] = y0
    ref[:, half : 2 * half] = y1
    for j in range(size.slots):
        ref[:, 2 * half + j * span : 2 * half + (j + 1) * span] = payload[j]


def stash_kernel(size, stash, squeeze, partial):
    ticks, rows, half = stash.shape
    whole = dot(stash[...].reshape(ticks * rows, half), squeeze[...], NT) * size.in_scale
    for t in range(ticks):
        partial[t] = whole[t * rows : (t + 1) * rows]


def keep(size, keep_mine, keep_other, x0, x1, ranks):
    keep_mine[0] = x0
    keep_other[0, :, : size.half] = x1
    keep_other[0, :, size.half :] = ranks


def keep_passed(size, ref, x0, x1, ranks):
    half, kept = size.half, size.kept
    for part, x in enumerate((x0, x1)):
        ref[part, :, :half] = x
        ref[part, :, half:kept] = ranks


def entering(place, size, step, x0, x1, where, feeds, at_end):
    index = where[4 + step]
    for n, ref in feeds.items():
        here = jnp.logical_and(at_end, index == n)
        x0 = jnp.where(here, ref[:, : size.half], x0)
        x1 = jnp.where(here, ref[:, size.half :], x1)
    return x0, x1


def first_kernel(size, where, x_in, again_own, mine, other, out, hist_mine, hist_other, keep_mine, keep_other, sems):
    place = Place(where)
    x0, x1, payload = read(size, x_in)
    y0, y1, ranks, payload = section_step(
        size, place, place.section, 0, x0, x1, again_own[0], payload, stacked(place, mine, other)
    )
    keep(size, keep_mine, keep_other, x0, x1, ranks)
    copies = [
        pltpu.make_async_copy(keep_mine, hist_mine.at[pl.ds(0, 1)], sems.at[0]),
        pltpu.make_async_copy(keep_other, hist_other.at[pl.ds(0, 1)], sems.at[1]),
    ]
    for copy in copies:
        copy.start()
    write(size, out, y0, y1, payload)
    for copy in copies:
        copy.wait()


def second_kernel(size, where, x_in, again_peer, squeeze0, squeeze1, expand0, expand1, out, held):
    place = Place(where)
    x0, x1, payload = read(size, x_in)
    y0, y1, ranks, sent = section_step(
        size, place, place.peer, 1, x0, x1, again_peer[0], payload,
        separate(place, squeeze0, squeeze1, expand0, expand1),
    )
    keep_passed(size, held, x0, x1, ranks)
    aligned = place.aligned
    sent = [jnp.where(aligned, sent[j], payload[j]) for j in range(size.slots)]
    write(size, out, jnp.where(aligned, y0, x0), jnp.where(aligned, y1, x1), sent)


def pair_kernel(size, step, turns, where, x_in, held, passed, again_own, again_peer, mine, other, *rest):
    feeds = dict(zip(turns, rest))
    _, _, out, held_out, passed_out, hist_mine, hist_other, keep_mine, keep_other, sems = rest[len(turns) :]
    half, kept = size.half, size.kept
    place = Place(where)
    aligned = place.aligned
    x0, x1, payload = read(size, x_in)
    x0, x1 = entering(place, size, step, x0, x1, where, feeds, place.at_end)
    tick = jnp.where(aligned, 2 * step, 2 * step - 1)
    again_peer = again_peer[jnp.where(aligned, step, step - 1)]
    own = again_own[2 * step]
    at_peer = jnp.where(aligned, 0, 2)
    y0, y1, ranks, payload = section_step(
        size, place, jnp.where(aligned, place.section, place.peer), tick, x0, x1,
        jnp.where(aligned, own, again_peer), payload, stacked(place, mine, other, at_peer),
    )
    z0, z1, ranks_b, sent = section_step(
        size, place, jnp.where(aligned, place.peer, place.section), tick + 1, y0, y1,
        jnp.where(aligned, again_peer, own), payload, stacked(place, mine, other, 2 - at_peer),
    )
    keep(
        size, keep_mine, keep_other,
        jnp.where(aligned, x0, y0), jnp.where(aligned, x1, y1), jnp.where(aligned, ranks, ranks_b),
    )
    copies = [
        pltpu.make_async_copy(keep_mine, hist_mine.at[pl.ds(step, 1)], sems.at[0]),
        pltpu.make_async_copy(keep_other, hist_other.at[pl.ds(step, 1)], sems.at[1]),
    ]
    for copy in copies:
        copy.start()
    final = step + 1 == size.steps
    for part, (first, second) in enumerate(((x0, y0), (x1, y1))):
        if not final:
            held_out[part, :, :half] = second
            held_out[part, :, half:] = ranks_b
        if step == 2:
            passed_out[0, part] = passed[0, part]
        at = passed_out.at[step - 1 if not final else 0, part]
        at[:, :half] = jnp.where(aligned, held[part, :, :half], first)
        at[:, half:] = jnp.where(aligned, held[part, :, half:], ranks)
    if final:
        held_out[...] = jnp.zeros(held_out.shape, held_out.dtype)
        sent = [jnp.where(aligned, payload[j], sent[j]) for j in range(size.slots)]
        z0, z1 = jnp.where(aligned, y0, z0), jnp.where(aligned, y1, z1)
    write(size, out, z0, z1, sent)
    for copy in copies:
        copy.wait()


def last_kernel(size, turns, where, x_in, again_own, mine, other, *rest):
    feeds = dict(zip(turns, rest))
    last_mine, last_other = rest[len(turns) :]
    half, kept = size.half, size.kept
    place = Place(where)
    x0, x1, payload = read(size, x_in)
    at_end = jnp.where(place.forward, place.section, place.sections - 1 - place.section) == 0
    x0, x1 = entering(place, size, size.steps, x0, x1, where, feeds, at_end)
    tick = size.ticks - 1
    y0, y1, ranks, _ = section_step(
        size, place, place.section, tick, x0, x1, again_own[tick], payload, stacked(place, mine, other)
    )
    for ref, x, y in ((last_mine, x0, y0), (last_other, x1, y1)):
        ref[:, :half] = x
        ref[:, half:kept] = ranks
        ref[:, kept:] = y


def end_kernel(size, where, mine, sent, got, odd, odd_got, late, late_got, last_mine, last_other, last_got, stash, *outs):
    squeeze_grad, expand_grad, fwd, bwd = outs
    ticks, half, kept, rank = size.ticks, size.half, size.kept, size.rank
    place = Place(where)

    def block(role, t, cols, part=0):
        here = place.role == role
        i = t // 2

        def pick(own, other):
            return jnp.where(here, own[:, cols], other[:, cols])

        if t % 2 == 0:
            return pick((mine, sent)[part].at[i], got.at[i])
        if t + 1 == ticks:
            return pick((last_mine, last_other)[part], last_got)
        if t + 3 == ticks:
            return pick(late.at[part], late_got)
        return pick(odd.at[i, part], odd_got.at[i])

    lag = 2 * (place.sections - 1 - place.section) + 1
    ranks = jnp.concatenate([block(1, t, slice(half, kept), 1) for t in range(ticks)], axis=0)
    regated, hidden_grad = ranks[:, :rank], ranks[:, rank:]
    for lo in range(0, half, CHUNK):
        cols = slice(lo, min(lo + CHUNK, half))
        a = [block(0, t, cols) for t in range(ticks - 1)]
        u = []
        for t in range(ticks):
            at = stash[t, :, cols]
            for j in range((t + 1) // 2):
                at = jnp.where(lag == 2 * j + 1, a[t - 2 * j - 1], at)
            u.append(at)
        u = jnp.concatenate(u, axis=0)
        g = jnp.concatenate([block(1, t, cols) for t in range(ticks)], axis=0)
        squeeze_grad[:, cols] = (dot(hidden_grad, u, TN) * size.in_scale).astype(jnp.bfloat16)
        expand_grad[:, cols] = (dot(regated, g, TN) * size.out_scale).astype(jnp.bfloat16)

    def carry(role):
        return jnp.where(place.role == role, last_mine[:, kept:], last_got[:, kept:])

    fwd[...] = carry(0)
    bwd[...] = carry(1)


def params():
    return pltpu.CompilerParams(vmem_limit_bytes=24 * 1024 * 1024)


def shape(*dims, dtype=jnp.bfloat16):
    return jax.ShapeDtypeStruct(dims, dtype)


def shards(
    activations,
    cotangent,
    squeeze_old,
    expand_old,
    squeeze_late,
    expand_late,
    stash_inputs,
    forward_in,
    backward_in,
):
    sections = lax.axis_size("pipe")
    replicas = lax.axis_size("dp")
    section = lax.axis_index("pipe")
    role = lax.axis_index("mp")
    half, rank = squeeze_old.shape[1], squeeze_old.shape[2]
    ticks, rows = stash_inputs.shape[2], stash_inputs.shape[3]
    size = Sizes(ticks, rows, rank, half)
    bf16, f32 = jnp.bfloat16, jnp.float32
    everyone = range(sections)

    def send(x, pairs):
        return lax.ppermute(x, ("pipe", "mp"), [(a * 2 + b, c * 2 + d) for (a, b), (c, d) in pairs])

    def swap(x):
        return lax.ppermute(x, "mp", [(0, 1), (1, 0)])

    def to_peer(x, senders):
        return send(x, [((s, c), (s ^ 1, c)) for s, c in senders])

    def tied(x, *others):
        return lax.optimization_barrier((x, *others))[0]

    def call(body, name, outs, in_specs, out_specs, scratch=(), aliases=None):
        return pl.pallas_call(
            functools.partial(body, size),
            out_shape=outs,
            in_specs=in_specs,
            out_specs=out_specs,
            scratch_shapes=list(scratch),
            input_output_aliases=aliases or {},
            compiler_params=params(),
            cost_estimate=pl.CostEstimate(
                flops=8 * rows * size.width * rank, bytes_accessed=8 * size.width * rank, transcendentals=0
            ),
            name=name,
        )

    side = section % 2
    where = jnp.stack([section, role, jnp.int32(sections), side]).astype(jnp.int32)
    forward = role == 0
    squeeze, expand = squeeze_old[0].T, expand_old[0]
    stash = stash_inputs[0, 0]
    fwd_in, bwd_in = forward_in[0, 0], backward_in[0, 0]
    acts, cots = activations[0], cotangent[0]
    both = [(s, c) for s in everyone for c in (0, 1)]

    squeeze_peer = to_peer(squeeze, both)
    expand_peer = to_peer(tied(expand, squeeze_peer), both)
    own = lax.optimization_barrier(jnp.stack([squeeze, expand]))
    other = swap(own)
    squeeze_peer_other, expand_peer_other = swap(squeeze_peer), swap(expand_peer)

    partial = call(
        stash_kernel, "stashed", shape(ticks, rows, rank, dtype=f32), [VMEM, VMEM], VMEM
    )(stash, squeeze)
    again_own = partial + swap(partial)
    again_peer = to_peer(again_own[1::2], [(s, 1) for s in everyone])

    cots_crossed = to_peer(cots, both)
    entering = jnp.concatenate([jnp.where(forward, acts, cots), swap(jnp.where(forward, cots, acts))], axis=1)
    crossed = jnp.concatenate([cots_crossed, swap(cots_crossed)], axis=1)
    crossed = jnp.where(forward, entering, crossed)
    per_tick = rows // acts.shape[0]

    ends = {}
    for b in range(ticks):
        to = b % 2 if b + 1 < ticks else 0
        ends.setdefault((to, 0), []).append(b)
        ends.setdefault((sections - 1 - to, 1), []).append(b)
    turn = {}
    trips = [[] for _ in range(ticks)]
    for (to, core), blocks in ends.items():
        seen = {0: 0, 1: 0}
        for b in blocks:
            at = [b * per_tick + m for m in range(per_tick)]
            crosses = int(core == 1 and b > 1 and not all(i == to for i in at))
            at = [i ^ crosses for i in at]
            if all(i == to for i in at):
                turn[to, core, b] = 1 - crosses
                continue
            n = seen[crosses]
            seen[crosses] += 1
            trip, swapped = crosses + n // 2, n % 2
            turn[to, core, b] = 2 + 2 * trip + swapped
            trips[trip].append((at, core, (to, core ^ swapped)))

    def fed(trip, rows_of):
        pieces = []
        for m in range(per_tick):
            moves = [((at[m], core), to) for at, core, to in trip]
            came = send(rows_of, [(a, b) for a, b in moves if a != b])
            for a, b in moves:
                if a == b:
                    came = jnp.where(jnp.logical_and(section == a[0], role == a[1]), rows_of, came)
            pieces.append(came)
        return jnp.concatenate(pieces, axis=0)

    feeds = [jnp.tile(crossed, (per_tick, 1)), jnp.tile(entering, (per_tick, 1))]
    for n, trip in enumerate(trips):
        if trip:
            feeds.append(fed(trip, crossed if n else entering))
            feeds.append(swap(feeds[-1]))

    def used(b_of):
        turns = {turn[to, core, b_of(to, core)] for (to, core), blocks in ends.items() if b_of(to, core) in blocks}
        return tuple(sorted(turns))

    def block_at(step):
        def b_of(to, core):
            side_to = to if core == 0 else sections - 1 - to
            return ticks - 1 if step == size.steps else 2 * step - side_to

        return b_of

    def reads(b_of):
        index = jnp.int32(0)
        for (to, core), blocks in ends.items():
            b = b_of(to, core)
            if b in blocks:
                here = jnp.logical_and(section == to, role == core)
                index = jnp.where(here, jnp.int32(turn[to, core, b]), index)
        return index

    where = jnp.concatenate([where, jnp.stack([reads(block_at(step)) for step in range(size.steps + 1)])])
    first_end = section == jnp.where(forward, 0, sections - 1)
    first_feed = feeds[1]
    for n in used(block_at(0)):
        first_feed = jnp.where(where[4] == n, feeds[n], first_feed)
    x = jnp.concatenate([jnp.where(forward, fwd_in, bwd_in), swap(jnp.where(forward, bwd_in, fwd_in))], axis=1)
    x = jnp.concatenate([jnp.where(first_end, first_feed, x), jnp.zeros((rows, size.message - size.width), bf16)], axis=1)

    hist_shapes = (shape(size.steps, rows, half), shape(size.steps, rows, size.kept))
    odd_shape = (2, rows, size.kept)
    keep_own = (
        pltpu.VMEM((1, rows, half), bf16),
        pltpu.VMEM((1, rows, size.kept), bf16),
        pltpu.SemaphoreType.DMA((2,)),
    )

    def averaged(old, late):
        if replicas == 2:
            total = late.astype(f32) + lax.ppermute(late, "dp", [(0, 1), (1, 0)]).astype(f32)
        else:
            total = lax.psum(late, "dp").astype(f32)
        return (old.astype(f32) - STEP_RATE * total / replicas).astype(bf16)

    squeeze_new = averaged(squeeze, squeeze_late[0, 0].T)
    expand_new = averaged(expand, expand_late[0, 0])

    ring = (
        [((s, 0), (s + 2, 0)) for s in range(sections - 2)]
        + [((sections - 2, 0), (sections - 1, 1)), ((sections - 1, 0), (sections - 2, 1))]
        + [((s, 1), (s - 2, 1)) for s in range(2, sections)]
    )
    ring_last = (
        [((s, 0), (s + 1, 0)) for s in range(sections - 1)]
        + [((sections - 1, 0), (sections - 1, 1))]
        + [((s, 1), (s - 1, 1)) for s in range(1, sections)]
    )
    def passing(slot):
        return [(s, c) for s, c in both if c == 1 or sections - 1 - (s ^ 1) + slot < size.slots - 1]

    x, hist_mine, hist_other = call(
        first_kernel, "first", (shape(rows, size.message), *hist_shapes),
        [SMEM, VMEM, VMEM, VMEM, VMEM], (VMEM, ANY, ANY), keep_own,
    )(where, x, again_own, own, other)
    x, held = call(
        second_kernel, "second", (shape(rows, size.message), shape(*odd_shape)),
        [SMEM] + [VMEM] * 6, (VMEM, VMEM),
    )(where, tied(x, *feeds[2::2]), again_peer, squeeze_peer, squeeze_peer_other, expand_peer, expand_peer_other)
    mine_all = jnp.concatenate([own, squeeze_peer[None], expand_peer[None]], axis=0)
    other_all = jnp.concatenate([other, squeeze_peer_other[None], expand_peer_other[None]], axis=0)
    x = send(x, ring)
    passed = jnp.zeros((1, *odd_shape), bf16)
    for step in range(1, size.steps):
        final = step + 1 == size.steps
        if step == 2:
            x = tied(x, squeeze_new)
        if step == 3:
            x = tied(x, expand_new)
        turns = used(block_at(step))
        body = functools.partial(lambda step, turns, size, *refs: pair_kernel(size, step, turns, *refs), step, turns)
        x, held, passed_now, hist_mine, hist_other = call(
            body, f"pair{step}",
            (
                shape(rows, size.message),
                shape(*((8, 128) if final else odd_shape)),
                shape(1 if final else step, *odd_shape),
                *hist_shapes,
            ),
            [SMEM] + [VMEM] * (7 + len(turns)) + [ANY] * 2, (VMEM, VMEM, VMEM, ANY, ANY), keep_own,
            {8 + len(turns): 3, 9 + len(turns): 4},
        )(
            where, x, held, passed, again_own, again_peer, mine_all, other_all, *(feeds[n] for n in turns),
            hist_mine, hist_other,
        )
        x = send(x, ring_last if final else ring)
        if final:
            odd, late = to_peer(passed, passing(0)), to_peer(passed_now[0], passing(size.steps - 2))
        passed = passed_now
    odd_got, late_got = swap(odd[:, 1]), swap(late[1])
    hist_got = swap(hist_other)
    turns = used(block_at(size.steps))
    last_mine, last_other = call(
        functools.partial(lambda turns, size, *refs: last_kernel(size, turns, *refs), turns), "last",
        (shape(rows, size.kept + half), shape(rows, size.kept + half)),
        [SMEM] + [VMEM] * (4 + len(turns)), (VMEM, VMEM),
    )(where, tied(x, odd), again_own, own, other, *(feeds[n] for n in turns))
    last_got = swap(last_other)
    squeeze_grad, expand_grad, fwd_carry, bwd_carry = call(
        end_kernel, "finish",
        (shape(rank, half), shape(rank, half), shape(rows, half), shape(rows, half)),
        [SMEM] + [VMEM] * 11, (VMEM,) * 4,
    )(where, hist_mine, hist_other, hist_got, odd, odd_got, late, late_got, last_mine, last_other, last_got, stash)
    return (
        squeeze_new.T[None],
        expand_new[None],
        squeeze_grad.T[None, None],
        expand_grad[None, None],
        fwd_carry[None, None],
        bwd_carry[None, None],
    )


def solution(mesh):
    placed = (
        P("dp", "pipe", "mp"),
        P("dp", "pipe", "mp"),
        P("pipe", "mp", None),
        P("pipe", None, "mp"),
        P("dp", "pipe", "mp", None),
        P("dp", "pipe", None, "mp"),
        P("dp", "pipe", None, None, "mp"),
        P("dp", "pipe", None, "mp"),
        P("dp", "pipe", None, "mp"),
    )
    return jax.shard_map(
        shards,
        mesh=mesh,
        in_specs=placed,
        out_specs=(
            P("pipe", "mp", None),
            P("pipe", None, "mp"),
            P("dp", "pipe", "mp", None),
            P("dp", "pipe", None, "mp"),
            P("dp", "pipe", None, "mp"),
            P("dp", "pipe", None, "mp"),
        ),
        check_vma=False,
    )
```

```python
import functools
import math

import jax
import jax.numpy as jnp
from jax import lax
from jax.experimental import pallas as pl
from jax.experimental.pallas import tpu as pltpu
from jax.sharding import PartitionSpec as P

BRANCH_SCALE = 0.25
STEP_RATE = 0.5
CHUNK = 512

VMEM = pl.BlockSpec(memory_space=pltpu.VMEM)
SMEM = pl.BlockSpec(memory_space=pltpu.SMEM)
ANY = pl.BlockSpec(memory_space=pl.ANY)
NT = (((1,), (1,)), ((), ()))
TN = (((0,), (0,)), ((), ()))


def dot(a, b, dims=(((1,), (0,)), ((), ()))):
    return lax.dot_general(a, b, dims, preferred_element_type=jnp.float32)


def gelu_and_slope(x):
    c = math.sqrt(2.0 / math.pi)
    t = jnp.tanh(c * (x + 0.044715 * (x * x * x)))
    half = 0.5 * (1.0 + t)
    slope = half + 0.5 * x * (1.0 - t * t) * (c * (1.0 + 3 * 0.044715 * (x * x)))
    return x * half, slope


def split_words(x):
    hi = x.astype(jnp.bfloat16)
    lo = (x - hi.astype(jnp.float32)).astype(jnp.bfloat16)
    return jnp.concatenate([hi, lo], axis=1)


def join_words(words):
    rank = words.shape[1] // 2
    return words[:, :rank].astype(jnp.float32) + words[:, rank:].astype(jnp.float32)


class Place:
    def __init__(self, where):
        self.section, self.role, self.sections = where[0], where[1], where[2]
        self.side = where[3]
        self.forward = self.role == 0
        self.aligned = self.side == self.role
        self.peer = self.section + 1 - 2 * self.side
        pair = jnp.where(self.forward, self.section, self.sections - 1 - self.section)
        self.at_end = pair < 2


class Sizes:
    def __init__(self, ticks, rows, rank, half):
        self.ticks, self.rows, self.rank, self.half = ticks, rows, rank, half
        self.steps = ticks // 2
        self.slots = ticks // 2
        self.width = 2 * half
        self.message = 2 * half + self.slots * 2 * rank
        self.kept = half + 2 * rank
        self.in_scale = 1.0 / math.sqrt(2 * half)
        self.out_scale = BRANCH_SCALE / math.sqrt(rank)


def stacked(place, mine, other, at=0):
    into, out = at + place.role, at + 1 - place.role
    return (lambda: mine[into]), (lambda: other[into]), (lambda: mine[out]), (lambda: other[out])


def separate(place, squeeze0, squeeze1, expand0, expand1):
    def either(a, b):
        return lambda: jnp.where(place.forward, a[...], b[...])

    return either(squeeze0, expand0), either(squeeze1, expand1), either(expand0, squeeze0), either(expand1, squeeze1)


def section_step(size, place, section, tick, x0, x1, again, payload, weights):
    forward = place.forward
    back = place.sections - 1 - section
    into0, into1, from0, from1 = weights
    h = (dot(x0, into0(), NT) + dot(x1, into1(), NT)) * jnp.where(
        forward, size.in_scale, size.out_scale
    )
    for j in range(size.slots):
        ready = jnp.logical_and(back == j, tick >= 2 * j + 1)
        again = jnp.where(ready, join_words(payload[j]), again)
    value, slope = gelu_and_slope(jnp.where(forward, h, again))
    z = jnp.where(forward, value, h * slope).astype(jnp.bfloat16)
    ranks = jnp.concatenate([value.astype(jnp.bfloat16), z], axis=1)
    scale = jnp.where(forward, size.out_scale, size.in_scale)
    y0 = (x0.astype(jnp.float32) + dot(z, from0()) * scale).astype(jnp.bfloat16)
    y1 = (x1.astype(jnp.float32) + dot(z, from1()) * scale).astype(jnp.bfloat16)
    words = split_words(h)
    payload = [jnp.where(jnp.logical_and(forward, back == j), words, payload[j]) for j in range(size.slots)]
    return y0, y1, ranks, payload


def read(size, ref):
    half, span = size.half, 2 * size.rank
    payload = [ref[:, 2 * half + j * span : 2 * half + (j + 1) * span] for j in range(size.slots)]
    return ref[:, :half], ref[:, half : 2 * half], payload


def write(size, ref, y0, y1, payload):
    half, span = size.half, 2 * size.rank
    ref[:, :half] = y0
    ref[:, half : 2 * half] = y1
    for j in range(size.slots):
        ref[:, 2 * half + j * span : 2 * half + (j + 1) * span] = payload[j]


def stash_kernel(size, stash, squeeze, partial):
    ticks, rows, half = stash.shape
    whole = dot(stash[...].reshape(ticks * rows, half), squeeze[...], NT) * size.in_scale
    for t in range(ticks):
        partial[t] = whole[t * rows : (t + 1) * rows]


def keep(size, keep_mine, keep_other, x0, x1, ranks):
    keep_mine[0] = x0
    keep_other[0, :, : size.half] = x1
    keep_other[0, :, size.half :] = ranks


def keep_passed(size, ref, x0, x1, ranks):
    half, kept = size.half, size.kept
    for part, x in enumerate((x0, x1)):
        ref[part, :, :half] = x
        ref[part, :, half:kept] = ranks


def entering(place, size, step, x0, x1, where, feeds, at_end):
    index = where[4 + step]
    for n, ref in feeds.items():
        here = jnp.logical_and(at_end, index == n)
        x0 = jnp.where(here, ref[:, : size.half], x0)
        x1 = jnp.where(here, ref[:, size.half :], x1)
    return x0, x1


def first_kernel(size, where, x_in, again_own, mine, other, out, hist_mine, hist_other, keep_mine, keep_other, sems):
    place = Place(where)
    x0, x1, payload = read(size, x_in)
    y0, y1, ranks, payload = section_step(
        size, place, place.section, 0, x0, x1, again_own[0], payload, stacked(place, mine, other)
    )
    keep(size, keep_mine, keep_other, x0, x1, ranks)
    copies = [
        pltpu.make_async_copy(keep_mine, hist_mine.at[pl.ds(0, 1)], sems.at[0]),
        pltpu.make_async_copy(keep_other, hist_other.at[pl.ds(0, 1)], sems.at[1]),
    ]
    for copy in copies:
        copy.start()
    write(size, out, y0, y1, payload)
    for copy in copies:
        copy.wait()


def second_kernel(size, where, x_in, again_peer, squeeze0, squeeze1, expand0, expand1, out, held):
    place = Place(where)
    x0, x1, payload = read(size, x_in)
    y0, y1, ranks, sent = section_step(
        size, place, place.peer, 1, x0, x1, again_peer[0], payload,
        separate(place, squeeze0, squeeze1, expand0, expand1),
    )
    keep_passed(size, held, x0, x1, ranks)
    aligned = place.aligned
    sent = [jnp.where(aligned, sent[j], payload[j]) for j in range(size.slots)]
    write(size, out, jnp.where(aligned, y0, x0), jnp.where(aligned, y1, x1), sent)


def pair_kernel(size, step, turns, where, x_in, held, passed, again_own, again_peer, mine, other, *rest):
    feeds = dict(zip(turns, rest))
    _, _, out, held_out, passed_out, hist_mine, hist_other, keep_mine, keep_other, sems = rest[len(turns) :]
    half, kept = size.half, size.kept
    place = Place(where)
    aligned = place.aligned
    x0, x1, payload = read(size, x_in)
    x0, x1 = entering(place, size, step, x0, x1, where, feeds, place.at_end)
    tick = jnp.where(aligned, 2 * step, 2 * step - 1)
    again_peer = again_peer[jnp.where(aligned, step, step - 1)]
    own = again_own[2 * step]
    at_peer = jnp.where(aligned, 0, 2)
    y0, y1, ranks, payload = section_step(
        size, place, jnp.where(aligned, place.section, place.peer), tick, x0, x1,
        jnp.where(aligned, own, again_peer), payload, stacked(place, mine, other, at_peer),
    )
    z0, z1, ranks_b, sent = section_step(
        size, place, jnp.where(aligned, place.peer, place.section), tick + 1, y0, y1,
        jnp.where(aligned, again_peer, own), payload, stacked(place, mine, other, 2 - at_peer),
    )
    keep(
        size, keep_mine, keep_other,
        jnp.where(aligned, x0, y0), jnp.where(aligned, x1, y1), jnp.where(aligned, ranks, ranks_b),
    )
    copies = [
        pltpu.make_async_copy(keep_mine, hist_mine.at[pl.ds(step, 1)], sems.at[0]),
        pltpu.make_async_copy(keep_other, hist_other.at[pl.ds(step, 1)], sems.at[1]),
    ]
    for copy in copies:
        copy.start()
    final = step + 1 == size.steps
    for part, (first, second) in enumerate(((x0, y0), (x1, y1))):
        if not final:
            held_out[part, :, :half] = second
            held_out[part, :, half:] = ranks_b
        if step == 2:
            passed_out[0, part] = passed[0, part]
        at = passed_out.at[step - 1 if not final else 0, part]
        at[:, :half] = jnp.where(aligned, held[part, :, :half], first)
        at[:, half:] = jnp.where(aligned, held[part, :, half:], ranks)
    if final:
        held_out[...] = jnp.zeros(held_out.shape, held_out.dtype)
        sent = [jnp.where(aligned, payload[j], sent[j]) for j in range(size.slots)]
        z0, z1 = jnp.where(aligned, y0, z0), jnp.where(aligned, y1, z1)
    write(size, out, z0, z1, sent)
    for copy in copies:
        copy.wait()


def last_kernel(size, turns, where, x_in, again_own, mine, other, *rest):
    feeds = dict(zip(turns, rest))
    last_mine, last_other = rest[len(turns) :]
    half, kept = size.half, size.kept
    place = Place(where)
    x0, x1, payload = read(size, x_in)
    at_end = jnp.where(place.forward, place.section, place.sections - 1 - place.section) == 0
    x0, x1 = entering(place, size, size.steps, x0, x1, where, feeds, at_end)
    tick = size.ticks - 1
    y0, y1, ranks, _ = section_step(
        size, place, place.section, tick, x0, x1, again_own[tick], payload, stacked(place, mine, other)
    )
    for ref, x, y in ((last_mine, x0, y0), (last_other, x1, y1)):
        ref[:, :half] = x
        ref[:, half:kept] = ranks
        ref[:, kept:] = y


def end_kernel(size, where, mine, sent, got, odd, odd_got, late, late_got, last_mine, last_other, last_got, stash, *outs):
    squeeze_grad, expand_grad, fwd, bwd = outs
    ticks, half, kept, rank = size.ticks, size.half, size.kept, size.rank
    place = Place(where)

    def block(role, t, cols, part=0):
        here = place.role == role
        i = t // 2

        def pick(own, other):
            return jnp.where(here, own[:, cols], other[:, cols])

        if t % 2 == 0:
            return pick((mine, sent)[part].at[i], got.at[i])
        if t + 1 == ticks:
            return pick((last_mine, last_other)[part], last_got)
        if t + 3 == ticks:
            return pick(late.at[part], late_got)
        return pick(odd.at[i, part], odd_got.at[i])

    lag = 2 * (place.sections - 1 - place.section) + 1
    ranks = jnp.concatenate([block(1, t, slice(half, kept), 1) for t in range(ticks)], axis=0)
    regated, hidden_grad = ranks[:, :rank], ranks[:, rank:]
    for lo in range(0, half, CHUNK):
        cols = slice(lo, min(lo + CHUNK, half))
        a = [block(0, t, cols) for t in range(ticks - 1)]
        u = []
        for t in range(ticks):
            at = stash[t, :, cols]
            for j in range((t + 1) // 2):
                at = jnp.where(lag == 2 * j + 1, a[t - 2 * j - 1], at)
            u.append(at)
        u = jnp.concatenate(u, axis=0)
        g = jnp.concatenate([block(1, t, cols) for t in range(ticks)], axis=0)
        squeeze_grad[:, cols] = (dot(hidden_grad, u, TN) * size.in_scale).astype(jnp.bfloat16)
        expand_grad[:, cols] = (dot(regated, g, TN) * size.out_scale).astype(jnp.bfloat16)

    def carry(role):
        return jnp.where(place.role == role, last_mine[:, kept:], last_got[:, kept:])

    fwd[...] = carry(0)
    bwd[...] = carry(1)


def params():
    return pltpu.CompilerParams(vmem_limit_bytes=24 * 1024 * 1024)


def shape(*dims, dtype=jnp.bfloat16):
    return jax.ShapeDtypeStruct(dims, dtype)


def shards(
    activations,
    cotangent,
    squeeze_old,
    expand_old,
    squeeze_late,
    expand_late,
    stash_inputs,
    forward_in,
    backward_in,
):
    sections = lax.axis_size("pipe")
    replicas = lax.axis_size("dp")
    section = lax.axis_index("pipe")
    role = lax.axis_index("mp")
    half, rank = squeeze_old.shape[1], squeeze_old.shape[2]
    ticks, rows = stash_inputs.shape[2], stash_inputs.shape[3]
    size = Sizes(ticks, rows, rank, half)
    bf16, f32 = jnp.bfloat16, jnp.float32
    everyone = range(sections)

    def send(x, pairs):
        return lax.ppermute(x, ("pipe", "mp"), [(a * 2 + b, c * 2 + d) for (a, b), (c, d) in pairs])

    def swap(x):
        return lax.ppermute(x, "mp", [(0, 1), (1, 0)])

    def to_peer(x, senders):
        return send(x, [((s, c), (s ^ 1, c)) for s, c in senders])

    def tied(x, *others):
        return lax.optimization_barrier((x, *others))[0]

    def call(body, name, outs, in_specs, out_specs, scratch=(), aliases=None):
        return pl.pallas_call(
            functools.partial(body, size),
            out_shape=outs,
            in_specs=in_specs,
            out_specs=out_specs,
            scratch_shapes=list(scratch),
            input_output_aliases=aliases or {},
            compiler_params=params(),
            cost_estimate=pl.CostEstimate(
                flops=8 * rows * size.width * rank, bytes_accessed=8 * size.width * rank, transcendentals=0
            ),
            name=name,
        )

    side = section % 2
    where = jnp.stack([section, role, jnp.int32(sections), side]).astype(jnp.int32)
    forward = role == 0
    squeeze, expand = squeeze_old[0].T, expand_old[0]
    stash = stash_inputs[0, 0]
    fwd_in, bwd_in = forward_in[0, 0], backward_in[0, 0]
    acts, cots = activations[0], cotangent[0]
    both = [(s, c) for s in everyone for c in (0, 1)]

    def averaged(old, late, came):
        total = late.astype(f32) + came.astype(f32) if replicas == 2 else came.astype(f32)
        return (old.astype(f32) - STEP_RATE * total / replicas).astype(bf16)

    def across(late):
        return lax.ppermute(late, "dp", [(0, 1), (1, 0)]) if replicas == 2 else lax.psum(late, "dp")

    squeeze_late, expand_late = squeeze_late[0, 0].T, expand_late[0, 0]
    squeeze_peer = to_peer(squeeze, both)
    expand_peer = to_peer(tied(expand, squeeze_peer), both)
    squeeze_peer_other = swap(squeeze_peer)
    squeeze_came = across(tied(squeeze_late, squeeze_peer_other))
    expand_came = across(tied(expand_late, squeeze_peer_other))
    squeeze_new = averaged(squeeze, squeeze_late, squeeze_came)
    expand_new = averaged(expand, expand_late, expand_came)
    own = lax.optimization_barrier(jnp.stack([squeeze, expand]))
    other = swap(own)

    partial = call(
        stash_kernel, "stashed", shape(ticks, rows, rank, dtype=f32), [VMEM, VMEM], VMEM
    )(stash, squeeze)
    again_own = partial + swap(partial)
    again_peer = to_peer(tied(again_own[1::2], squeeze_peer_other), [(s, 1) for s in everyone])

    cots_crossed = to_peer(cots, both)
    entering = jnp.concatenate([jnp.where(forward, acts, cots), swap(jnp.where(forward, cots, acts))], axis=1)
    crossed = jnp.concatenate([cots_crossed, swap(cots_crossed)], axis=1)
    crossed = jnp.where(forward, entering, crossed)
    per_tick = rows // acts.shape[0]

    ends = {}
    for b in range(ticks):
        to = b % 2 if b + 1 < ticks else 0
        ends.setdefault((to, 0), []).append(b)
        ends.setdefault((sections - 1 - to, 1), []).append(b)
    turn = {}
    trips = [[] for _ in range(ticks)]
    for (to, core), blocks in ends.items():
        seen = {0: 0, 1: 0}
        for b in blocks:
            at = [b * per_tick + m for m in range(per_tick)]
            crosses = int(core == 1 and b > 1 and not all(i == to for i in at))
            at = [i ^ crosses for i in at]
            if all(i == to for i in at):
                turn[to, core, b] = 1 - crosses
                continue
            n = seen[crosses]
            seen[crosses] += 1
            trip, swapped = crosses + n // 2, n % 2
            turn[to, core, b] = 2 + 2 * trip + swapped
            trips[trip].append((at, core, (to, core ^ swapped)))

    def fed(trip, rows_of):
        pieces = []
        for m in range(per_tick):
            moves = [((at[m], core), to) for at, core, to in trip]
            came = send(rows_of, [(a, b) for a, b in moves if a != b])
            for a, b in moves:
                if a == b:
                    came = jnp.where(jnp.logical_and(section == a[0], role == a[1]), rows_of, came)
            pieces.append(came)
        return jnp.concatenate(pieces, axis=0)

    feeds = [jnp.tile(crossed, (per_tick, 1)), jnp.tile(entering, (per_tick, 1))]
    for n, trip in enumerate(trips):
        if trip:
            feeds.append(fed(trip, crossed if n else tied(entering, squeeze_peer)))
            feeds.append(swap(feeds[-1]))

    def used(b_of):
        turns = {turn[to, core, b_of(to, core)] for (to, core), blocks in ends.items() if b_of(to, core) in blocks}
        return tuple(sorted(turns))

    def block_at(step):
        def b_of(to, core):
            side_to = to if core == 0 else sections - 1 - to
            return ticks - 1 if step == size.steps else 2 * step - side_to

        return b_of

    def reads(b_of):
        index = jnp.int32(0)
        for (to, core), blocks in ends.items():
            b = b_of(to, core)
            if b in blocks:
                here = jnp.logical_and(section == to, role == core)
                index = jnp.where(here, jnp.int32(turn[to, core, b]), index)
        return index

    where = jnp.concatenate([where, jnp.stack([reads(block_at(step)) for step in range(size.steps + 1)])])
    first_end = section == jnp.where(forward, 0, sections - 1)
    first_feed = feeds[1]
    for n in used(block_at(0)):
        first_feed = jnp.where(where[4] == n, feeds[n], first_feed)
    x = jnp.concatenate([jnp.where(forward, fwd_in, bwd_in), swap(jnp.where(forward, bwd_in, fwd_in))], axis=1)
    x = jnp.concatenate([jnp.where(first_end, first_feed, x), jnp.zeros((rows, size.message - size.width), bf16)], axis=1)

    hist_shapes = (shape(size.steps, rows, half), shape(size.steps, rows, size.kept))
    odd_shape = (2, rows, size.kept)
    keep_own = (
        pltpu.VMEM((1, rows, half), bf16),
        pltpu.VMEM((1, rows, size.kept), bf16),
        pltpu.SemaphoreType.DMA((2,)),
    )

    ring = (
        [((s, 0), (s + 2, 0)) for s in range(sections - 2)]
        + [((sections - 2, 0), (sections - 1, 1)), ((sections - 1, 0), (sections - 2, 1))]
        + [((s, 1), (s - 2, 1)) for s in range(2, sections)]
    )
    ring_last = (
        [((s, 0), (s + 1, 0)) for s in range(sections - 1)]
        + [((sections - 1, 0), (sections - 1, 1))]
        + [((s, 1), (s - 1, 1)) for s in range(1, sections)]
    )
    def passing(slot):
        return [(s, c) for s, c in both if c == 1 or sections - 1 - (s ^ 1) + slot < size.slots - 1]

    x, hist_mine, hist_other = call(
        first_kernel, "first", (shape(rows, size.message), *hist_shapes),
        [SMEM, VMEM, VMEM, VMEM, VMEM], (VMEM, ANY, ANY), keep_own,
    )(where, x, again_own, own, other)
    expand_peer_other = swap(tied(expand_peer, x))
    x, held = call(
        second_kernel, "second", (shape(rows, size.message), shape(*odd_shape)),
        [SMEM] + [VMEM] * 6, (VMEM, VMEM),
    )(where, tied(x, *feeds[2::2]), again_peer, squeeze_peer, squeeze_peer_other, expand_peer, expand_peer_other)
    mine_all = jnp.concatenate([own, squeeze_peer[None], expand_peer[None]], axis=0)
    other_all = jnp.concatenate([other, squeeze_peer_other[None], expand_peer_other[None]], axis=0)
    x = send(x, ring)
    passed = jnp.zeros((1, *odd_shape), bf16)
    for step in range(1, size.steps):
        final = step + 1 == size.steps
        if step == 2:
            x = tied(x, squeeze_new)
        if step == 3:
            x = tied(x, expand_new)
        turns = used(block_at(step))
        body = functools.partial(lambda step, turns, size, *refs: pair_kernel(size, step, turns, *refs), step, turns)
        x, held, passed_now, hist_mine, hist_other = call(
            body, f"pair{step}",
            (
                shape(rows, size.message),
                shape(*((8, 128) if final else odd_shape)),
                shape(1 if final else step, *odd_shape),
                *hist_shapes,
            ),
            [SMEM] + [VMEM] * (7 + len(turns)) + [ANY] * 2, (VMEM, VMEM, VMEM, ANY, ANY), keep_own,
            {8 + len(turns): 3, 9 + len(turns): 4},
        )(
            where, x, held, passed, again_own, again_peer, mine_all, other_all, *(feeds[n] for n in turns),
            hist_mine, hist_other,
        )
        x = send(x, ring_last if final else ring)
        if final:
            odd, late = to_peer(passed, passing(0)), to_peer(passed_now[0], passing(size.steps - 2))
        passed = passed_now
    odd_got, late_got = swap(odd[:, 1]), swap(late[1])
    hist_got = swap(hist_other)
    turns = used(block_at(size.steps))
    last_mine, last_other = call(
        functools.partial(lambda turns, size, *refs: last_kernel(size, turns, *refs), turns), "last",
        (shape(rows, size.kept + half), shape(rows, size.kept + half)),
        [SMEM] + [VMEM] * (4 + len(turns)), (VMEM, VMEM),
    )(where, tied(x, odd), again_own, own, other, *(feeds[n] for n in turns))
    last_got = swap(last_other)
    squeeze_grad, expand_grad, fwd_carry, bwd_carry = call(
        end_kernel, "finish",
        (shape(rank, half), shape(rank, half), shape(rows, half), shape(rows, half)),
        [SMEM] + [VMEM] * 11, (VMEM,) * 4,
    )(where, hist_mine, hist_other, hist_got, odd, odd_got, late, late_got, last_mine, last_other, last_got, stash)
    return (
        squeeze_new.T[None],
        expand_new[None],
        squeeze_grad.T[None, None],
        expand_grad[None, None],
        fwd_carry[None, None],
        bwd_carry[None, None],
    )


def solution(mesh):
    placed = (
        P("dp", "pipe", "mp"),
        P("dp", "pipe", "mp"),
        P("pipe", "mp", None),
        P("pipe", None, "mp"),
        P("dp", "pipe", "mp", None),
        P("dp", "pipe", None, "mp"),
        P("dp", "pipe", None, None, "mp"),
        P("dp", "pipe", None, "mp"),
        P("dp", "pipe", None, "mp"),
    )
    return jax.shard_map(
        shards,
        mesh=mesh,
        in_specs=placed,
        out_specs=(
            P("pipe", "mp", None),
            P("pipe", None, "mp"),
            P("dp", "pipe", "mp", None),
            P("dp", "pipe", None, "mp"),
            P("dp", "pipe", None, "mp"),
            P("dp", "pipe", None, "mp"),
        ),
        check_vma=False,
    )
```

```python
import functools
import math

import jax
import jax.numpy as jnp
from jax import lax
from jax.experimental import pallas as pl
from jax.experimental.pallas import tpu as pltpu
from jax.sharding import PartitionSpec as P

BRANCH_SCALE = 0.25
STEP_RATE = 0.5
CHUNK = 512

VMEM = pl.BlockSpec(memory_space=pltpu.VMEM)
SMEM = pl.BlockSpec(memory_space=pltpu.SMEM)
ANY = pl.BlockSpec(memory_space=pl.ANY)
NT = (((1,), (1,)), ((), ()))
TN = (((0,), (0,)), ((), ()))


def dot(a, b, dims=(((1,), (0,)), ((), ()))):
    return lax.dot_general(a, b, dims, preferred_element_type=jnp.float32)


def gelu_and_slope(x):
    c = math.sqrt(2.0 / math.pi)
    t = jnp.tanh(c * (x + 0.044715 * (x * x * x)))
    half = 0.5 * (1.0 + t)
    slope = half + 0.5 * x * (1.0 - t * t) * (c * (1.0 + 3 * 0.044715 * (x * x)))
    return x * half, slope


def split_words(x):
    hi = x.astype(jnp.bfloat16)
    lo = (x - hi.astype(jnp.float32)).astype(jnp.bfloat16)
    return jnp.concatenate([hi, lo], axis=1)


def join_words(words):
    rank = words.shape[1] // 2
    return words[:, :rank].astype(jnp.float32) + words[:, rank:].astype(jnp.float32)


class Place:
    def __init__(self, where):
        self.section, self.role, self.sections = where[0], where[1], where[2]
        self.side = where[3]
        self.forward = self.role == 0
        self.aligned = self.side == self.role
        self.peer = self.section + 1 - 2 * self.side
        pair = jnp.where(self.forward, self.section, self.sections - 1 - self.section)
        self.at_end = pair < 2


class Sizes:
    def __init__(self, ticks, rows, rank, half):
        self.ticks, self.rows, self.rank, self.half = ticks, rows, rank, half
        self.steps = ticks // 2
        self.slots = ticks // 2
        self.width = 2 * half
        self.message = 2 * half + self.slots * 2 * rank
        self.kept = half + 2 * rank
        self.in_scale = 1.0 / math.sqrt(2 * half)
        self.out_scale = BRANCH_SCALE / math.sqrt(rank)


def stacked(place, mine, other, at=0):
    into, out = at + place.role, at + 1 - place.role
    return (lambda: mine[into]), (lambda: other[into]), (lambda: mine[out]), (lambda: other[out])


def separate(place, squeeze0, squeeze1, expand0, expand1):
    def either(a, b):
        return lambda: jnp.where(place.forward, a[...], b[...])

    return either(squeeze0, expand0), either(squeeze1, expand1), either(expand0, squeeze0), either(expand1, squeeze1)


def section_step(size, place, section, tick, x0, x1, again, payload, weights):
    forward = place.forward
    back = place.sections - 1 - section
    into0, into1, from0, from1 = weights
    h = (dot(x0, into0(), NT) + dot(x1, into1(), NT)) * jnp.where(
        forward, size.in_scale, size.out_scale
    )
    for j in range(size.slots):
        ready = jnp.logical_and(back == j, tick >= 2 * j + 1)
        again = jnp.where(ready, join_words(payload[j]), again)
    value, slope = gelu_and_slope(jnp.where(forward, h, again))
    z = jnp.where(forward, value, h * slope).astype(jnp.bfloat16)
    ranks = jnp.concatenate([value.astype(jnp.bfloat16), z], axis=1)
    scale = jnp.where(forward, size.out_scale, size.in_scale)
    y0 = (x0.astype(jnp.float32) + dot(z, from0()) * scale).astype(jnp.bfloat16)
    y1 = (x1.astype(jnp.float32) + dot(z, from1()) * scale).astype(jnp.bfloat16)
    words = split_words(h)
    payload = [jnp.where(jnp.logical_and(forward, back == j), words, payload[j]) for j in range(size.slots)]
    return y0, y1, ranks, payload


def read(size, ref):
    half, span = size.half, 2 * size.rank
    payload = [ref[:, 2 * half + j * span : 2 * half + (j + 1) * span] for j in range(size.slots)]
    return ref[:, :half], ref[:, half : 2 * half], payload


def write(size, ref, y0, y1, payload):
    half, span = size.half, 2 * size.rank
    ref[:, :half] = y0
    ref[:, half : 2 * half] = y1
    for j in range(size.slots):
        ref[:, 2 * half + j * span : 2 * half + (j + 1) * span] = payload[j]


def stash_kernel(size, stash, squeeze, partial):
    ticks, rows, half = stash.shape
    whole = dot(stash[...].reshape(ticks * rows, half), squeeze[...], NT) * size.in_scale
    for t in range(ticks):
        partial[t] = whole[t * rows : (t + 1) * rows]


def keep(size, keep_mine, keep_other, x0, x1, ranks):
    keep_mine[0] = x0
    keep_other[0, :, : size.half] = x1
    keep_other[0, :, size.half :] = ranks


def keep_passed(size, ref, x0, x1, ranks):
    half, kept = size.half, size.kept
    for part, x in enumerate((x0, x1)):
        ref[part, :, :half] = x
        ref[part, :, half:kept] = ranks


def entering(place, size, step, x0, x1, where, feeds, at_end):
    index = where[4 + step]
    for n, ref in feeds.items():
        here = jnp.logical_and(at_end, index == n)
        x0 = jnp.where(here, ref[:, : size.half], x0)
        x1 = jnp.where(here, ref[:, size.half :], x1)
    return x0, x1


def first_kernel(size, where, x_in, again_own, mine, other, out, hist_mine, hist_other, keep_mine, keep_other, sems):
    place = Place(where)
    x0, x1, payload = read(size, x_in)
    y0, y1, ranks, payload = section_step(
        size, place, place.section, 0, x0, x1, again_own[0], payload, stacked(place, mine, other)
    )
    keep(size, keep_mine, keep_other, x0, x1, ranks)
    copies = [
        pltpu.make_async_copy(keep_mine, hist_mine.at[pl.ds(0, 1)], sems.at[0]),
        pltpu.make_async_copy(keep_other, hist_other.at[pl.ds(0, 1)], sems.at[1]),
    ]
    for copy in copies:
        copy.start()
    write(size, out, y0, y1, payload)
    for copy in copies:
        copy.wait()


def second_kernel(size, where, x_in, again_peer, squeeze0, squeeze1, expand0, expand1, out, held):
    place = Place(where)
    x0, x1, payload = read(size, x_in)
    y0, y1, ranks, sent = section_step(
        size, place, place.peer, 1, x0, x1, again_peer[0], payload,
        separate(place, squeeze0, squeeze1, expand0, expand1),
    )
    keep_passed(size, held, x0, x1, ranks)
    aligned = place.aligned
    sent = [jnp.where(aligned, sent[j], payload[j]) for j in range(size.slots)]
    write(size, out, jnp.where(aligned, y0, x0), jnp.where(aligned, y1, x1), sent)


def pair_kernel(size, step, turns, where, x_in, held, passed, again_own, again_peer, mine, other, *rest):
    feeds = dict(zip(turns, rest))
    _, _, out, held_out, passed_out, hist_mine, hist_other, keep_mine, keep_other, sems = rest[len(turns) :]
    half, kept = size.half, size.kept
    place = Place(where)
    aligned = place.aligned
    x0, x1, payload = read(size, x_in)
    x0, x1 = entering(place, size, step, x0, x1, where, feeds, place.at_end)
    tick = jnp.where(aligned, 2 * step, 2 * step - 1)
    again_peer = again_peer[jnp.where(aligned, step, step - 1)]
    own = again_own[2 * step]
    at_peer = jnp.where(aligned, 0, 2)
    y0, y1, ranks, payload = section_step(
        size, place, jnp.where(aligned, place.section, place.peer), tick, x0, x1,
        jnp.where(aligned, own, again_peer), payload, stacked(place, mine, other, at_peer),
    )
    z0, z1, ranks_b, sent = section_step(
        size, place, jnp.where(aligned, place.peer, place.section), tick + 1, y0, y1,
        jnp.where(aligned, again_peer, own), payload, stacked(place, mine, other, 2 - at_peer),
    )
    keep(
        size, keep_mine, keep_other,
        jnp.where(aligned, x0, y0), jnp.where(aligned, x1, y1), jnp.where(aligned, ranks, ranks_b),
    )
    copies = [
        pltpu.make_async_copy(keep_mine, hist_mine.at[pl.ds(step, 1)], sems.at[0]),
        pltpu.make_async_copy(keep_other, hist_other.at[pl.ds(step, 1)], sems.at[1]),
    ]
    for copy in copies:
        copy.start()
    final = step + 1 == size.steps
    for part, (first, second) in enumerate(((x0, y0), (x1, y1))):
        if not final:
            held_out[part, :, :half] = second
            held_out[part, :, half:] = ranks_b
        if step == 2:
            passed_out[0, part] = passed[0, part]
        at = passed_out.at[step - 1 if not final else 0, part]
        at[:, :half] = jnp.where(aligned, held[part, :, :half], first)
        at[:, half:] = jnp.where(aligned, held[part, :, half:], ranks)
    if final:
        held_out[...] = jnp.zeros(held_out.shape, held_out.dtype)
        sent = [jnp.where(aligned, payload[j], sent[j]) for j in range(size.slots)]
        z0, z1 = jnp.where(aligned, y0, z0), jnp.where(aligned, y1, z1)
    write(size, out, z0, z1, sent)
    for copy in copies:
        copy.wait()


def last_kernel(size, turns, where, x_in, again_own, mine, other, *rest):
    feeds = dict(zip(turns, rest))
    last_mine, last_other = rest[len(turns) :]
    half, kept = size.half, size.kept
    place = Place(where)
    x0, x1, payload = read(size, x_in)
    at_end = jnp.where(place.forward, place.section, place.sections - 1 - place.section) == 0
    x0, x1 = entering(place, size, size.steps, x0, x1, where, feeds, at_end)
    tick = size.ticks - 1
    y0, y1, ranks, _ = section_step(
        size, place, place.section, tick, x0, x1, again_own[tick], payload, stacked(place, mine, other)
    )
    for ref, x, y in ((last_mine, x0, y0), (last_other, x1, y1)):
        ref[:, :half] = x
        ref[:, half:kept] = ranks
        ref[:, kept:] = y


def end_kernel(size, where, mine, sent, got, odd, odd_got, late, late_got, last_mine, last_other, last_got, stash, *outs):
    squeeze_grad, expand_grad, fwd, bwd = outs
    ticks, half, kept, rank = size.ticks, size.half, size.kept, size.rank
    place = Place(where)

    def block(role, t, cols, part=0):
        here = place.role == role
        i = t // 2

        def pick(own, other):
            return jnp.where(here, own[:, cols], other[:, cols])

        if t % 2 == 0:
            return pick((mine, sent)[part].at[i], got.at[i])
        if t + 1 == ticks:
            return pick((last_mine, last_other)[part], last_got)
        if t + 3 == ticks:
            return pick(late.at[part], late_got)
        return pick(odd.at[i, part], odd_got.at[i])

    lag = 2 * (place.sections - 1 - place.section) + 1
    ranks = jnp.concatenate([block(1, t, slice(half, kept), 1) for t in range(ticks)], axis=0)
    regated, hidden_grad = ranks[:, :rank], ranks[:, rank:]
    for lo in range(0, half, CHUNK):
        cols = slice(lo, min(lo + CHUNK, half))
        a = [block(0, t, cols) for t in range(ticks - 1)]
        u = []
        for t in range(ticks):
            at = stash[t, :, cols]
            for j in range((t + 1) // 2):
                at = jnp.where(lag == 2 * j + 1, a[t - 2 * j - 1], at)
            u.append(at)
        u = jnp.concatenate(u, axis=0)
        g = jnp.concatenate([block(1, t, cols) for t in range(ticks)], axis=0)
        squeeze_grad[:, cols] = (dot(hidden_grad, u, TN) * size.in_scale).astype(jnp.bfloat16)
        expand_grad[:, cols] = (dot(regated, g, TN) * size.out_scale).astype(jnp.bfloat16)

    def carry(role):
        return jnp.where(place.role == role, last_mine[:, kept:], last_got[:, kept:])

    fwd[...] = carry(0)
    bwd[...] = carry(1)


def params():
    return pltpu.CompilerParams(vmem_limit_bytes=24 * 1024 * 1024)


def shape(*dims, dtype=jnp.bfloat16):
    return jax.ShapeDtypeStruct(dims, dtype)


def shards(
    activations,
    cotangent,
    squeeze_old,
    expand_old,
    squeeze_late,
    expand_late,
    stash_inputs,
    forward_in,
    backward_in,
):
    sections = lax.axis_size("pipe")
    replicas = lax.axis_size("dp")
    section = lax.axis_index("pipe")
    role = lax.axis_index("mp")
    half, rank = squeeze_old.shape[1], squeeze_old.shape[2]
    ticks, rows = stash_inputs.shape[2], stash_inputs.shape[3]
    size = Sizes(ticks, rows, rank, half)
    bf16, f32 = jnp.bfloat16, jnp.float32
    everyone = range(sections)

    def send(x, pairs):
        return lax.ppermute(x, ("pipe", "mp"), [(a * 2 + b, c * 2 + d) for (a, b), (c, d) in pairs])

    def swap(x):
        return lax.ppermute(x, "mp", [(0, 1), (1, 0)])

    def to_peer(x, senders):
        return send(x, [((s, c), (s ^ 1, c)) for s, c in senders])

    def tied(x, *others):
        return lax.optimization_barrier((x, *others))[0]

    def call(body, name, outs, in_specs, out_specs, scratch=(), aliases=None):
        return pl.pallas_call(
            functools.partial(body, size),
            out_shape=outs,
            in_specs=in_specs,
            out_specs=out_specs,
            scratch_shapes=list(scratch),
            input_output_aliases=aliases or {},
            compiler_params=params(),
            cost_estimate=pl.CostEstimate(
                flops=8 * rows * size.width * rank, bytes_accessed=8 * size.width * rank, transcendentals=0
            ),
            name=name,
        )

    side = section % 2
    where = jnp.stack([section, role, jnp.int32(sections), side]).astype(jnp.int32)
    forward = role == 0
    squeeze, expand = squeeze_old[0].T, expand_old[0]
    stash = stash_inputs[0, 0]
    fwd_in, bwd_in = forward_in[0, 0], backward_in[0, 0]
    acts, cots = activations[0], cotangent[0]
    both = [(s, c) for s in everyone for c in (0, 1)]

    def averaged(old, late, came):
        total = late.astype(f32) + came.astype(f32) if replicas == 2 else came.astype(f32)
        return (old.astype(f32) - STEP_RATE * total / replicas).astype(bf16)

    def across(late):
        return lax.ppermute(late, "dp", [(0, 1), (1, 0)]) if replicas == 2 else lax.psum(late, "dp")

    squeeze_late, expand_late = squeeze_late[0, 0].T, expand_late[0, 0]
    squeeze_peer = to_peer(squeeze, both)
    expand_peer = to_peer(tied(expand, squeeze_peer), both)
    squeeze_peer_other = swap(squeeze_peer)
    squeeze_came = across(tied(squeeze_late, squeeze_peer))
    expand_came = across(tied(expand_late, squeeze_peer))
    squeeze_new = averaged(squeeze, squeeze_late, squeeze_came)
    expand_new = averaged(expand, expand_late, expand_came)
    own = lax.optimization_barrier(jnp.stack([squeeze, expand]))
    other = swap(own)

    partial = call(
        stash_kernel, "stashed", shape(ticks, rows, rank, dtype=f32), [VMEM, VMEM], VMEM
    )(stash, squeeze)
    again_own = partial + swap(partial)
    again_peer = to_peer(tied(again_own[1::2], squeeze_peer), [(s, 1) for s in everyone])

    cots_crossed = to_peer(cots, both)
    entering = jnp.concatenate([jnp.where(forward, acts, cots), swap(jnp.where(forward, cots, acts))], axis=1)
    crossed = jnp.concatenate([cots_crossed, swap(cots_crossed)], axis=1)
    crossed = jnp.where(forward, entering, crossed)
    per_tick = rows // acts.shape[0]

    ends = {}
    for b in range(ticks):
        to = b % 2 if b + 1 < ticks else 0
        ends.setdefault((to, 0), []).append(b)
        ends.setdefault((sections - 1 - to, 1), []).append(b)
    turn = {}
    trips = [[] for _ in range(ticks)]
    for (to, core), blocks in ends.items():
        seen = {0: 0, 1: 0}
        for b in blocks:
            at = [b * per_tick + m for m in range(per_tick)]
            crosses = int(core == 1 and b > 1 and not all(i == to for i in at))
            at = [i ^ crosses for i in at]
            if all(i == to for i in at):
                turn[to, core, b] = 1 - crosses
                continue
            n = seen[crosses]
            seen[crosses] += 1
            trip, swapped = crosses + n // 2, n % 2
            turn[to, core, b] = 2 + 2 * trip + swapped
            trips[trip].append((at, core, (to, core ^ swapped)))

    def fed(trip, rows_of):
        pieces = []
        for m in range(per_tick):
            moves = [((at[m], core), to) for at, core, to in trip]
            came = send(rows_of, [(a, b) for a, b in moves if a != b])
            for a, b in moves:
                if a == b:
                    came = jnp.where(jnp.logical_and(section == a[0], role == a[1]), rows_of, came)
            pieces.append(came)
        return jnp.concatenate(pieces, axis=0)

    feeds = [jnp.tile(crossed, (per_tick, 1)), jnp.tile(entering, (per_tick, 1))]
    for n, trip in enumerate(trips):
        if trip:
            feeds.append(fed(trip, crossed if n else tied(entering, squeeze_peer)))
            feeds.append(swap(feeds[-1]))

    def used(b_of):
        turns = {turn[to, core, b_of(to, core)] for (to, core), blocks in ends.items() if b_of(to, core) in blocks}
        return tuple(sorted(turns))

    def block_at(step):
        def b_of(to, core):
            side_to = to if core == 0 else sections - 1 - to
            return ticks - 1 if step == size.steps else 2 * step - side_to

        return b_of

    def reads(b_of):
        index = jnp.int32(0)
        for (to, core), blocks in ends.items():
            b = b_of(to, core)
            if b in blocks:
                here = jnp.logical_and(section == to, role == core)
                index = jnp.where(here, jnp.int32(turn[to, core, b]), index)
        return index

    where = jnp.concatenate([where, jnp.stack([reads(block_at(step)) for step in range(size.steps + 1)])])
    first_end = section == jnp.where(forward, 0, sections - 1)
    first_feed = feeds[1]
    for n in used(block_at(0)):
        first_feed = jnp.where(where[4] == n, feeds[n], first_feed)
    x = jnp.concatenate([jnp.where(forward, fwd_in, bwd_in), swap(jnp.where(forward, bwd_in, fwd_in))], axis=1)
    x = jnp.concatenate([jnp.where(first_end, first_feed, x), jnp.zeros((rows, size.message - size.width), bf16)], axis=1)

    hist_shapes = (shape(size.steps, rows, half), shape(size.steps, rows, size.kept))
    odd_shape = (2, rows, size.kept)
    keep_own = (
        pltpu.VMEM((1, rows, half), bf16),
        pltpu.VMEM((1, rows, size.kept), bf16),
        pltpu.SemaphoreType.DMA((2,)),
    )

    ring = (
        [((s, 0), (s + 2, 0)) for s in range(sections - 2)]
        + [((sections - 2, 0), (sections - 1, 1)), ((sections - 1, 0), (sections - 2, 1))]
        + [((s, 1), (s - 2, 1)) for s in range(2, sections)]
    )
    ring_last = (
        [((s, 0), (s + 1, 0)) for s in range(sections - 1)]
        + [((sections - 1, 0), (sections - 1, 1))]
        + [((s, 1), (s - 1, 1)) for s in range(1, sections)]
    )
    def passing(slot):
        return [(s, c) for s, c in both if c == 1 or sections - 1 - (s ^ 1) + slot < size.slots - 1]

    x, hist_mine, hist_other = call(
        first_kernel, "first", (shape(rows, size.message), *hist_shapes),
        [SMEM, VMEM, VMEM, VMEM, VMEM], (VMEM, ANY, ANY), keep_own,
    )(where, x, again_own, own, other)
    expand_peer_other = swap(tied(expand_peer, x))
    x, held = call(
        second_kernel, "second", (shape(rows, size.message), shape(*odd_shape)),
        [SMEM] + [VMEM] * 6, (VMEM, VMEM),
    )(where, tied(x, *feeds[2::2]), again_peer, squeeze_peer, squeeze_peer_other, expand_peer, expand_peer_other)
    mine_all = jnp.concatenate([own, squeeze_peer[None], expand_peer[None]], axis=0)
    other_all = jnp.concatenate([other, squeeze_peer_other[None], expand_peer_other[None]], axis=0)
    x = send(x, ring)
    passed = jnp.zeros((1, *odd_shape), bf16)
    for step in range(1, size.steps):
        final = step + 1 == size.steps
        if step == 2:
            x = tied(x, squeeze_came, expand_came)
        if step == 3:
            x = tied(x, squeeze_new)
        turns = used(block_at(step))
        body = functools.partial(lambda step, turns, size, *refs: pair_kernel(size, step, turns, *refs), step, turns)
        x, held, passed_now, hist_mine, hist_other = call(
            body, f"pair{step}",
            (
                shape(rows, size.message),
                shape(*((8, 128) if final else odd_shape)),
                shape(1 if final else step, *odd_shape),
                *hist_shapes,
            ),
            [SMEM] + [VMEM] * (7 + len(turns)) + [ANY] * 2, (VMEM, VMEM, VMEM, ANY, ANY), keep_own,
            {8 + len(turns): 3, 9 + len(turns): 4},
        )(
            where, x, held, passed, again_own, again_peer, mine_all, other_all, *(feeds[n] for n in turns),
            hist_mine, hist_other,
        )
        x = send(x, ring_last if final else ring)
        if final:
            odd, late = to_peer(passed, passing(0)), to_peer(passed_now[0], passing(size.steps - 2))
        passed = passed_now
    odd_got, late_got = swap(odd[:, 1]), swap(late[1])
    hist_got = swap(hist_other)
    turns = used(block_at(size.steps))
    last_mine, last_other = call(
        functools.partial(lambda turns, size, *refs: last_kernel(size, turns, *refs), turns), "last",
        (shape(rows, size.kept + half), shape(rows, size.kept + half)),
        [SMEM] + [VMEM] * (4 + len(turns)), (VMEM, VMEM),
    )(where, tied(x, odd, expand_new), again_own, own, other, *(feeds[n] for n in turns))
    last_got = swap(last_other)
    squeeze_grad, expand_grad, fwd_carry, bwd_carry = call(
        end_kernel, "finish",
        (shape(rank, half), shape(rank, half), shape(rows, half), shape(rows, half)),
        [SMEM] + [VMEM] * 11, (VMEM,) * 4,
    )(where, hist_mine, hist_other, hist_got, odd, odd_got, late, late_got, last_mine, last_other, last_got, stash)
    return (
        squeeze_new.T[None],
        expand_new[None],
        squeeze_grad.T[None, None],
        expand_grad[None, None],
        fwd_carry[None, None],
        bwd_carry[None, None],
    )


def solution(mesh):
    placed = (
        P("dp", "pipe", "mp"),
        P("dp", "pipe", "mp"),
        P("pipe", "mp", None),
        P("pipe", None, "mp"),
        P("dp", "pipe", "mp", None),
        P("dp", "pipe", None, "mp"),
        P("dp", "pipe", None, None, "mp"),
        P("dp", "pipe", None, "mp"),
        P("dp", "pipe", None, "mp"),
    )
    return jax.shard_map(
        shards,
        mesh=mesh,
        in_specs=placed,
        out_specs=(
            P("pipe", "mp", None),
            P("pipe", None, "mp"),
            P("dp", "pipe", "mp", None),
            P("dp", "pipe", None, "mp"),
            P("dp", "pipe", None, "mp"),
            P("dp", "pipe", None, "mp"),
        ),
        check_vma=False,
    )
```
